256 devices in a mesh: light: 64 (over z, y, x_hi), depth: 2 (over core), tile: 2 (over x_lo).
Axes of the slice: x: 4 (x_hi: 2, x_lo: 2; x = x_hi * 2 + x_lo), y: 4, z: 8, core: 2. Of those that a mesh axis runs over, the one named last changes fastest.
Arguments:
- density: float32 [2048, 128, 1024], P('light', 'depth', 'tile'), may hold values from 0.05 to 2
- extinction: float32 [3], replicated, may hold values from 1 to 4
- sun_colour: float32 [3], replicated, may hold values from 1 to 3
- sky_colour: float32 [3], replicated, may hold values from 0.2 to 2
Outputs:
- image: float32 [3, 2048, 1024], P(None, ('light', 'depth'), 'tile')
- transmittance: float32 [3, 2048, 1024], P(None, ('light', 'depth'), 'tile')
The draws below stay inside these ranges and needn't reach their ends.
All inputs are finite; a program needn't handle non-finite values.
Results may differ from the reference program's by a relative error of at most 0.0003.
Values sent between devices are 32-bit elements; how exact they have to be, the bound alone decides.
No kernel may reach another device: no remote copies, remote signals or barrier semaphores. Data moves between devices by JAX's collectives and lax.ppermute only.
A program may use at most 64 MiB of HBM per device.

```python
import math
import jax
import jax.numpy as jnp
from jax import lax

BZ = 512
COLOURS = 3
NX = 2048
NY = 128
NZ = 1024


def levels(rng, extent, cuts, low, largest):
    factor_of, own = 1.0, jax.random.fold_in(rng, 6)
    for position, blocks in cuts:
        steps = jnp.exp(jax.random.uniform(jax.random.fold_in(own, position), (blocks,), jnp.float32, low / len(cuts), largest / len(cuts)))
        factor_of = factor_of * jnp.repeat(steps, extent[position] // blocks).reshape([-1 if axis == position else 1 for axis in range(len(extent))])
    return factor_of


def setup_inputs(seed: int = 0) -> dict:
    streams_of = jax.random.split(jax.random.key(seed), 5)
    return {
        "density": jnp.clip(jnp.exp(math.log(2.0) - 3.6888794 * jax.random.uniform(streams_of[0], (NX, NY, NZ), jnp.float32) ** levels(streams_of[0], (NX, NY, NZ), ((0, 64), (1, 2), (2, 2)), -0.2, 0.2)), 0.05, 2.0),
        "extinction": jnp.clip(jnp.exp(jax.random.uniform(streams_of[1], (COLOURS,), jnp.float32, math.log(1.0), math.log(4.0))), 1.0, 4.0),
        "sun_colour": jnp.clip(jax.random.uniform(streams_of[2], (COLOURS,), jnp.float32, 1.0, 3.0), 1.0, 3.0),
        "sky_colour": jnp.clip(jax.random.uniform(streams_of[3], (COLOURS,), jnp.float32, 0.2, 2.0), 0.2, 2.0),
    }


def render_block(block, extinction, sun_colour, sky_colour):
    full_x = block.shape[0]
    full_y = block.shape[1]
    sun_depth = (jnp.cumsum(block, axis=0) - 0.5 * block) / full_x
    view_depth = (jnp.cumsum(block, axis=1) - block) / full_y
    column_total = jnp.sum(block, axis=1) / full_y
    images = []
    passes = []
    for colour in range(3):
        radiance = sun_colour[colour] * jnp.exp(-extinction[colour] * sun_depth)
        opacity = -jnp.expm1(-extinction[colour] * block / full_y)
        weight = jnp.exp(-extinction[colour] * view_depth)
        summed = jnp.sum(weight * opacity * radiance, axis=1)
        passing = jnp.exp(-extinction[colour] * column_total)
        images.append(summed + sky_colour[colour] * passing)
        passes.append(passing)
    return jnp.stack(images), jnp.stack(passes)


def reference(density, extinction, sun_colour, sky_colour):
    width = BZ // max(1, BZ // 128)
    count = NZ // width

    def one_block(index):
        block = lax.dynamic_slice_in_dim(density, (index * width).astype(jnp.int32), width, 2)
        return render_block(block, extinction, sun_colour, sky_colour)

    images, passes = lax.map(one_block, jnp.arange(count, dtype=jnp.int32))
    image = jnp.transpose(images, (1, 2, 0, 3)).reshape(3, NX, NZ)
    transmittance = jnp.transpose(passes, (1, 2, 0, 3)).reshape(3, NX, NZ)
    return image, transmittance
```

```python
import functools

import jax
import jax.numpy as jnp
from jax import lax
from jax.experimental import pallas as pl
from jax.experimental.pallas import tpu as pltpu
from jax.sharding import Mesh
from jax.sharding import PartitionSpec as P

PLANE = ("y", "x")
LANES = 128
VMEM = pl.BlockSpec(memory_space=pltpu.VMEM)
SMEM = pl.BlockSpec(memory_space=pltpu.SMEM)


def params(mib):
    return pltpu.CompilerParams(vmem_limit_bytes=mib * 1024 * 1024)


def column_kernel(density_ref, sum_ref):
    @pl.when(pl.program_id(0) == 0)
    def _():
        sum_ref[...] = jnp.zeros_like(sum_ref)

    sum_ref[...] += jnp.sum(density_ref[...], axis=0)


def column_light_of(density):
    nx, ny, nz = density.shape
    chunk = 8
    return pl.pallas_call(
        column_kernel,
        grid=(nx // chunk,),
        in_specs=[pl.BlockSpec((chunk, ny, nz), lambda i: (i, 0, 0))],
        out_specs=pl.BlockSpec((ny, nz), lambda i: (0, 0)),
        out_shape=jax.ShapeDtypeStruct((ny, nz), jnp.float32),
        compiler_params=params(16),
        name="column_light",
    )(density)


def view_kernel(density_ref, sum_ref):
    sum_ref[...] = jnp.sum(density_ref[...], axis=1)


def column_view_of(density):
    nx, ny, nz = density.shape
    chunk = 8
    return pl.pallas_call(
        view_kernel,
        grid=(nx // chunk,),
        in_specs=[pl.BlockSpec((chunk, ny, nz), lambda i: (i, 0, 0))],
        out_specs=pl.BlockSpec((chunk, nz), lambda i: (i, 0)),
        out_shape=jax.ShapeDtypeStruct((nx, nz), jnp.float32),
        compiler_params=params(16),
        cost_estimate=pl.CostEstimate(flops=2**20, bytes_accessed=2**22, transcendentals=0),
        name="column_view",
    )(density)


def brick_kernel(sizes, ext_ref, front_ref, d_ref, g_ref, s_ref):
    nx, ny, full_x, full_y = sizes
    lanes = pl.ds(pl.multiple_of(pl.program_id(0) * LANES, LANES), LANES)

    def along_x(i, _):
        carry = jnp.zeros((8, LANES), jnp.float32)
        for x in range(nx):
            at = pl.ds(pl.multiple_of(x * ny + i * 8, 8), 8)
            cell = d_ref[at, :]
            s_ref[at, :] = carry + 0.5 * cell
            carry = carry + cell
        return 0

    lax.fori_loop(0, ny // 8, along_x, 0)

    def along_y(i, _):
        xs = pl.multiple_of(i * 8, 8)
        view = front_ref[pl.ds(xs, 8), :]
        passing = [jnp.exp(view * (-ext_ref[c] / full_y)) for c in range(3)]

        def cells(step, state):
            view, passing = state
            passing = list(passing)
            for k in range(8):
                y = step * 8 + k
                at = pl.ds(xs * ny + y, 8, stride=ny)
                view = view + d_ref[at, :]
                sun = s_ref[at, :]
                for c in range(3):
                    later = jnp.exp(view * (-ext_ref[c] / full_y))
                    g_ref[c, y, pl.ds(xs, 8), lanes] = (passing[c] - later) * jnp.exp(sun * (-ext_ref[c] / full_x))
                    passing[c] = later
            return view, tuple(passing)

        lax.fori_loop(0, ny // 8, cells, (view, tuple(passing)))
        return 0

    lax.fori_loop(0, nx // 8, along_y, 0)


def brick_light_of(density, front, extinction, full_x, full_y):
    nx, ny, nz = density.shape
    return pl.pallas_call(
        functools.partial(brick_kernel, (nx, ny, full_x, full_y)),
        grid=(nz // LANES,),
        in_specs=[
            SMEM,
            pl.BlockSpec((nx, LANES), lambda i: (0, i)),
            pl.BlockSpec((nx * ny, LANES), lambda i: (0, i)),
        ],
        out_specs=VMEM,
        out_shape=pltpu.VMEM((3, ny, nx, nz), jnp.float32),
        scratch_shapes=[pltpu.VMEM((nx * ny, LANES), jnp.float32)],
        compiler_params=params(16),
        cost_estimate=pl.CostEstimate(flops=2**25, bytes_accessed=2**24, transcendentals=6 * 2**20),
        name="brick_light",
    )(extinction, front, density.reshape(nx * ny, nz))


def pixel_kernel(sizes, half_ref, ext_ref, sun_ref, before_ref, g_ref, out_ref, a_ref):
    nx, ny, nz, full_x = sizes
    tiles = nz // LANES
    rows = nx // 2
    for c in range(3):
        a_ref[c] = sun_ref[c] * jnp.exp(before_ref[...] * (-ext_ref[c] / full_x))
    base = pl.multiple_of(half_ref[0] * rows, 8)

    def pixels(i, _):
        lanes = pl.ds(pl.multiple_of((i % tiles) * LANES, LANES), LANES)
        c = i // tiles
        total = [jnp.zeros((8, LANES), jnp.float32) for _ in range(rows // 8)]
        for y in range(ny):
            light = jnp.broadcast_to(a_ref[c, pl.ds(y, 1), lanes], (8, LANES))
            for t in range(rows // 8):
                total[t] = total[t] + light * g_ref[c, y, pl.ds(base + 8 * t, 8), lanes]
        for t in range(rows // 8):
            out_ref[c, 8 * t : 8 * t + 8, lanes] = total[t]
        return 0

    lax.fori_loop(0, 3 * tiles, pixels, 0)


def pixels_of(half, brick, before, extinction, sun_colour, full_x, name):
    _, ny, nx, nz = brick.shape
    return pl.pallas_call(
        functools.partial(pixel_kernel, (nx, ny, nz, full_x)),
        in_specs=[SMEM, SMEM, SMEM, VMEM, VMEM],
        out_specs=VMEM,
        out_shape=jax.ShapeDtypeStruct((3, nx // 2, nz), jnp.float32),
        scratch_shapes=[pltpu.VMEM((3, ny, nz), jnp.float32)],
        compiler_params=params(4),
        cost_estimate=pl.CostEstimate(flops=2**21, bytes_accessed=2**22, transcendentals=2**16),
        name=name,
    )(half, extinction, sun_colour, before, pltpu.with_memory_space_constraint(brick, pltpu.VMEM))


def light_before(column_light, sizes):
    planes, members = sizes
    ny, nz = column_light.shape
    part = ny // members
    own = lax.all_to_all(column_light.reshape(members, part, nz), PLANE, 0, 0, tiled=True)
    within = [jnp.zeros_like(own[0])]
    for k in range(members):
        within.append(within[-1] + own[k])
    plane_sum = within.pop()
    sums = lax.all_to_all(jnp.broadcast_to(plane_sum[None], (planes, part, nz)), "z", 0, 0, tiled=True)
    plane = lax.axis_index("z")
    nearer = jnp.zeros_like(plane_sum)
    for k in range(planes):
        nearer = nearer + jnp.where(k < plane, sums[k], 0.0)
    back = jnp.stack([value + nearer for value in within])
    return lax.all_to_all(back, PLANE, 0, 0, tiled=True).reshape(ny, nz)


def per_device(sizes, density, extinction, sun_colour, sky_colour):
    planes, members, full_x, full_y = sizes
    nx = density.shape[0]
    half = lax.axis_index("depth").astype(jnp.int32)
    swap = functools.partial(lax.ppermute, axis_name="depth", perm=[(0, 1), (1, 0)])
    column_light = column_light_of(density)
    before = light_before(column_light, (planes, members))
    column_view = column_view_of(density)
    other_view = swap(column_view)
    front = jnp.where(half == 1, other_view, 0.0)
    own_rows = lax.dynamic_slice_in_dim(column_view + other_view, half * (nx // 2), nx // 2, 0)
    transmittance = jnp.exp(-extinction[:, None, None] * own_rows[None] / full_y)
    background = sky_colour[:, None, None] * transmittance
    brick = brick_light_of(density, front, extinction, full_x, full_y)
    sent = pixels_of((1 - half).reshape(1), brick, before, extinction, sun_colour, full_x, "pixels_sent")
    received = swap(sent)
    kept = pixels_of(half.reshape(1), brick, before, extinction, sun_colour, full_x, "pixels_kept")
    return kept + received + background, transmittance


def solution(mesh):
    shape = (8, 4, 2, 2, 2)
    fine = Mesh(mesh.devices.reshape(shape), ("z", "y", "x", "depth", "tile"))
    light = ("z", "y", "x")
    sizes = (8, 8, 2048, 128)
    return jax.shard_map(
        functools.partial(per_device, sizes),
        mesh=fine,
        in_specs=(P(light, "depth", "tile"), P(), P(), P()),
        out_specs=(P(None, (*light, "depth"), "tile"), P(None, (*light, "depth"), "tile")),
        check_vma=False,
    )
```

```python
import functools

import jax
import jax.numpy as jnp
from jax import lax
from jax.experimental import pallas as pl
from jax.experimental.pallas import tpu as pltpu
from jax.sharding import PartitionSpec as P

LANES = 128
CHUNKS = 8
LOG2E = 1.4426950408889634
VMEM = pl.BlockSpec(memory_space=pltpu.VMEM)
HBM = pl.BlockSpec(memory_space=pltpu.HBM)


def params(mib):
    return pltpu.CompilerParams(vmem_limit_bytes=mib * 1024 * 1024)


def cost(flops, size, transcendentals=0):
    return pl.CostEstimate(flops=flops, bytes_accessed=size, transcendentals=transcendentals)


def load_kernel(sizes, density_ref, ext_ref, sun_ref, sky_ref, light_ref, view_ref, table_ref, held_ref, sums_ref, three_ref, sems, small_sems):
    nx, ny, full_x, full_y = sizes
    tiles = held_ref.shape[0]
    planes = nx // CHUNKS
    rows = planes * ny
    copies = [
        [
            pltpu.make_async_copy(
                density_ref.at[pl.ds(k * rows, rows), pl.ds(t * LANES, LANES)],
                held_ref.at[t, pl.ds(k * rows, rows)],
                sems.at[k, t],
            )
            for t in range(tiles)
        ]
        for k in range(CHUNKS)
    ]
    for chunk in copies:
        for copy in chunk:
            copy.start()
    small = [
        pltpu.make_async_copy(source, three_ref.at[i], small_sems.at[i]) for i, source in enumerate((ext_ref, sun_ref, sky_ref))
    ]
    for copy in small:
        copy.start()
    for k in range(CHUNKS):
        for t in range(tiles):
            copies[k][t].wait()
            block = held_ref[t, k * rows : (k + 1) * rows].reshape(planes, ny, LANES)
            part = jnp.sum(block, axis=0)
            sums_ref[t] = part if k == 0 else sums_ref[t] + part
            view_ref[k * planes : (k + 1) * planes, t * LANES : (t + 1) * LANES] = jnp.sum(block, axis=1)
    for t in range(tiles):
        light_ref[pl.ds(t, ny, stride=tiles), :] = sums_ref[t]
    for copy in small:
        copy.wait()
    for c in range(3):
        row = (-LOG2E / full_y * three_ref[0, c], -LOG2E / full_x * three_ref[0, c], three_ref[1, c], three_ref[2, c])
        for i, value in enumerate(row):
            table_ref[8 * (4 * c + i) : 8 * (4 * c + i) + 8] = jnp.full((8, LANES), value, jnp.float32)


def factor(table_ref, c, which):
    return table_ref[8 * (4 * c + which) : 8 * (4 * c + which) + 8]


def load_of(density, extinction, sun_colour, sky_colour, full_x, full_y):
    nx, ny, nz = density.shape
    tiles = nz // LANES
    return pl.pallas_call(
        functools.partial(load_kernel, (nx, ny, full_x, full_y)),
        in_specs=[HBM, HBM, HBM, HBM],
        out_specs=[VMEM, VMEM, VMEM],
        out_shape=[
            jax.ShapeDtypeStruct((ny * tiles, LANES), jnp.float32),
            jax.ShapeDtypeStruct((nx, nz), jnp.float32),
            jax.ShapeDtypeStruct((12 * 8, LANES), jnp.float32),
        ],
        scratch_shapes=[
            pltpu.VMEM((tiles, nx * ny, LANES), jnp.float32),
            pltpu.VMEM((tiles, ny, LANES), jnp.float32),
            pltpu.SMEM((3, 3), jnp.float32),
            pltpu.SemaphoreType.DMA((CHUNKS, tiles)),
            pltpu.SemaphoreType.DMA((3,)),
        ],
        compiler_params=params(8),
        cost_estimate=cost(2**21, 2**23),
        name="load",
    )(*(pltpu.with_memory_space_constraint(x, pltpu.HBM) for x in (density.reshape(nx * ny, nz), extinction, sun_colour, sky_colour)))


def before_kernel(each, own_ref, *refs):
    before_ref = refs[-1]
    upper = lax.broadcasted_iota(jnp.int32, (8, LANES), 0) >= each
    carry = jnp.zeros((8, LANES), jnp.float32)
    for k in range(own_ref.shape[0] // 8):
        block = own_ref[8 * k : 8 * k + 8]
        other = pltpu.roll(block, each, 0)
        before_ref[8 * k : 8 * k + 8] = carry + jnp.where(upper, other, 0.0)
        carry = carry + (block + other)


def before_of(own, each, after):
    return pl.pallas_call(
        functools.partial(before_kernel, each),
        in_specs=[VMEM] * (1 + len(after)),
        out_specs=VMEM,
        out_shape=jax.ShapeDtypeStruct(own.shape, jnp.float32),
        compiler_params=params(2),
        cost_estimate=cost(2**17, 2**26),
        name="before",
    )(own, *after)


def brick_kernel(nx, ny, table_ref, other_ref, d_ref, g_ref, done_ref, s_ref):
    behind = lax.axis_index("depth").astype(jnp.float32)
    done_ref[...] = jnp.zeros_like(done_ref)
    wide = 32

    def along_x(part, _):
        carry = jnp.zeros((wide, LANES), jnp.float32)
        for x in range(nx):
            at = pl.ds(pl.multiple_of(x * ny + part * wide, 8), wide)
            cell = d_ref[at, :]
            s_ref[at, :] = carry + 0.5 * cell
            carry = carry + cell
        return 0

    lax.fori_loop(0, ny // wide, along_x, 0)

    def along_y(i, _):
        xs = pl.multiple_of(i * 8, 8)
        view_rate = [factor(table_ref, c, 0) for c in range(3)]
        sun_rate = [factor(table_ref, c, 1) for c in range(3)]
        view = other_ref[pl.ds(xs, 8), :] * behind
        passing = [jnp.exp2(view * view_rate[c]) for c in range(3)]

        def cells(step, state):
            view, passing = state
            passing = list(passing)
            for k in range(8):
                y = step * 8 + k
                at = pl.ds(xs * ny + y, 8, stride=ny)
                view = view + d_ref[at, :]
                sun = s_ref[at, :]
                for c in range(3):
                    later = jnp.exp2(view * view_rate[c])
                    g_ref[0, c, y, pl.ds(xs, 8), :] = (passing[c] - later) * jnp.exp2(sun * sun_rate[c])
                    passing[c] = later
            return view, tuple(passing)

        lax.fori_loop(0, ny // 8, cells, (view, tuple(passing)))
        return 0

    lax.fori_loop(0, nx // 8, along_y, 0)


def brick_light_of(density, other_view, table):
    nx, ny, nz = density.shape
    return pl.pallas_call(
        functools.partial(brick_kernel, nx, ny),
        grid=(nz // LANES,),
        in_specs=[
            VMEM,
            pl.BlockSpec((nx, LANES), lambda i: (0, i)),
            pl.BlockSpec((nx * ny, LANES), lambda i: (0, i)),
        ],
        out_specs=[pl.BlockSpec((1, 3, ny, nx, LANES), lambda i: (i, 0, 0, 0, 0)), VMEM],
        out_shape=[
            pltpu.HBM((nz // LANES, 3, ny, nx, LANES), jnp.float32),
            jax.ShapeDtypeStruct((8, LANES), jnp.float32),
        ],
        scratch_shapes=[pltpu.VMEM((nx * ny, LANES), jnp.float32)],
        compiler_params=params(16),
        cost_estimate=cost(2**25, 2**24, 6 * 2**20),
        name="brick_light",
    )(table, other_view, pltpu.with_memory_space_constraint(density.reshape(nx * ny, nz), pltpu.HBM))


def sky_kernel(table_ref, view_ref, other_ref, passed_ref, behind_ref):
    _, rows, nz = passed_ref.shape
    start = lax.axis_index("depth") * rows
    for row in range(0, rows, 8):
        at = pl.ds(pl.multiple_of(start + row, 8), 8)
        for lane in range(0, nz, LANES):
            column = view_ref[at, lane : lane + LANES] + other_ref[at, lane : lane + LANES]
            for c in range(3):
                passed = jnp.exp2(column * factor(table_ref, c, 0))
                passed_ref[c, row : row + 8, lane : lane + LANES] = passed
                behind_ref[c, row : row + 8, lane : lane + LANES] = factor(table_ref, c, 3) * passed


def sky_of(view, other, table):
    nx, nz = view.shape
    shape = jax.ShapeDtypeStruct((3, nx // 2, nz), jnp.float32)
    return pl.pallas_call(
        sky_kernel,
        in_specs=[VMEM, VMEM, VMEM],
        out_specs=[VMEM, VMEM],
        out_shape=[shape, shape],
        compiler_params=params(2),
        name="sky",
    )(table, view, other)


def pixel_kernel(own, table_ref, before_ref, *refs):
    g_ref, start_ref, out_ref, a_ref = refs[0], refs[1:-2], refs[-2], refs[-1]
    tiles, _, ny, nx, _ = g_ref.shape
    rows = nx // 2
    for c in range(3):
        rate, colour = factor(table_ref, c, 1), factor(table_ref, c, 2)
        for row in range(0, before_ref.shape[0], 8):
            a_ref[c, row : row + 8] = colour * jnp.exp2(before_ref[row : row + 8] * rate)
    half = lax.axis_index("depth")
    base = pl.multiple_of((half if own else 1 - half) * rows, 8)
    ways = 4
    for tile in range(tiles):
        at = slice(tile * LANES, (tile + 1) * LANES)

        def pixels(c, _, tile=tile, at=at):
            total = [jnp.zeros((rows, LANES), jnp.float32) for _ in range(ways)]
            for y in range(ny):
                light = jnp.broadcast_to(a_ref[c, pl.ds(y * tiles + tile, 1), :], (rows, LANES))
                total[y % ways] = total[y % ways] + light * g_ref[tile, c, y, pl.ds(base, rows), :]
            value = (total[0] + total[1]) + (total[2] + total[3])
            out_ref[c, :, at] = value + start_ref[0][c, :, at] if start_ref else value
            return 0

        lax.fori_loop(0, 3, pixels, 0)


def pixels_of(own, brick, before, table, name, *start):
    tiles, _, ny, nx, _ = brick.shape
    return pl.pallas_call(
        functools.partial(pixel_kernel, own),
        in_specs=[VMEM] * (3 + len(start)),
        out_specs=VMEM,
        out_shape=jax.ShapeDtypeStruct((3, nx // 2, tiles * LANES), jnp.float32),
        scratch_shapes=[pltpu.VMEM((3, *before.shape), jnp.float32)],
        compiler_params=params(2),
        cost_estimate=cost(2**21, 2**22, 2**16),
        name=name,
    )(table, before, brick, *start)


def per_device(sizes, density, extinction, sun_colour, sky_colour):
    full_x, full_y = sizes
    nx, ny, nz = density.shape
    tiles = nz // LANES
    swap = functools.partial(lax.ppermute, axis_name="depth", perm=[(0, 1), (1, 0)])
    deal = functools.partial(lax.all_to_all, axis_name="light", split_axis=0, concat_axis=0, tiled=True)
    column_light, column_view, table = load_of(density, extinction, sun_colour, sky_colour, full_x, full_y)
    own = deal(column_light.reshape(ny, tiles, LANES)).reshape(ny * tiles, LANES)
    other_view = swap(column_view)
    transmittance, background = sky_of(column_view, other_view, table)
    brick, done = brick_light_of(density, other_view, table)
    before = deal(before_of(own, tiles, (done, background)).reshape(ny, tiles, LANES)).reshape(ny * tiles, LANES)
    sent = pixels_of(False, brick, before, table, "pixels_sent")
    received = swap(sent)
    kept = pixels_of(True, brick, before, table, "pixels_kept", background)
    return kept + received, transmittance


def solution(mesh):
    light = mesh.shape["light"]
    depth = mesh.shape["depth"]

    def render(density, extinction, sun_colour, sky_colour):
        full_x, full_y, _ = density.shape
        return jax.shard_map(
            functools.partial(per_device, (full_x, full_y)),
            mesh=mesh,
            in_specs=(P("light", "depth", "tile"), P(), P(), P()),
            out_specs=(P(None, ("light", "depth"), "tile"), P(None, ("light", "depth"), "tile")),
            check_vma=False,
        )(density, extinction, sun_colour, sky_colour)

    assert light == 64 and depth == 2
    return render
```

```python
import functools

import jax
import jax.numpy as jnp
from jax import lax
from jax.experimental import pallas as pl
from jax.experimental.pallas import tpu as pltpu
from jax.sharding import Mesh
from jax.sharding import PartitionSpec as P

LANES = 128
CHUNKS = 8
PIECES = 2
LOG2E = 1.4426950408889634
VMEM = pl.BlockSpec(memory_space=pltpu.VMEM)
HBM = pl.BlockSpec(memory_space=pltpu.HBM)
PLANE = ("y", "x")


def params(mib):
    return pltpu.CompilerParams(vmem_limit_bytes=mib * 1024 * 1024)


def cost(flops, size, transcendentals=0):
    return pl.CostEstimate(flops=flops, bytes_accessed=size, transcendentals=transcendentals)


def in_hbm(*arrays):
    return [pltpu.with_memory_space_constraint(x, pltpu.HBM) for x in arrays]


def load_kernel(sizes, density_ref, ext_ref, sun_ref, sky_ref, light_ref, table_ref, held_ref, three_ref, sems, small_sems):
    nx, full_x, full_y = sizes
    planes = nx // CHUNKS
    copies = [
        pltpu.make_async_copy(density_ref.at[pl.ds(k * planes, planes)], held_ref.at[pl.ds(k * planes, planes)], sems.at[k])
        for k in range(CHUNKS)
    ]
    small = [
        pltpu.make_async_copy(source, three_ref.at[i], small_sems.at[i]) for i, source in enumerate((ext_ref, sun_ref, sky_ref))
    ]
    for copy in (*copies, *small):
        copy.start()
    for k in range(CHUNKS):
        copies[k].wait()
        part = held_ref[k * planes]
        for x in range(k * planes + 1, (k + 1) * planes):
            part = part + held_ref[x]
        light_ref[...] = part if k == 0 else light_ref[...] + part
    for copy in small:
        copy.wait()
    for c in range(3):
        row = (-LOG2E / full_y * three_ref[0, c], -LOG2E / full_x * three_ref[0, c], three_ref[1, c], three_ref[2, c])
        for i, value in enumerate(row):
            table_ref[8 * (4 * c + i) : 8 * (4 * c + i) + 8] = jnp.full((8, LANES), value, jnp.float32)


def factor(table_ref, c, which):
    return table_ref[8 * (4 * c + which) : 8 * (4 * c + which) + 8]


def load_of(density, extinction, sun_colour, sky_colour, full_x, full_y):
    nx, ny, nz = density.shape
    return pl.pallas_call(
        functools.partial(load_kernel, (nx, full_x, full_y)),
        in_specs=[HBM, HBM, HBM, HBM],
        out_specs=[VMEM, VMEM],
        out_shape=[
            jax.ShapeDtypeStruct((ny, nz), jnp.float32),
            jax.ShapeDtypeStruct((12 * 8, LANES), jnp.float32),
        ],
        scratch_shapes=[
            pltpu.VMEM((nx, ny, nz), jnp.float32),
            pltpu.SMEM((3, 3), jnp.float32),
            pltpu.SemaphoreType.DMA((CHUNKS,)),
            pltpu.SemaphoreType.DMA((3,)),
        ],
        compiler_params=params(8),
        cost_estimate=cost(2**21, 2**23),
        name="load",
    )(*in_hbm(density, extinction, sun_colour, sky_colour))


def plane_kernel(own_ref, *refs):
    within_ref, sums_ref = refs[-2], refs[-1]
    members, part, _ = own_ref.shape
    total = jnp.zeros_like(own_ref[0])
    for k in range(members):
        within_ref[k] = total
        total = total + own_ref[k]
    for k in range(sums_ref.shape[0]):
        sums_ref[k] = total


def plane_of(own, planes, after):
    members, part, nz = own.shape
    return pl.pallas_call(
        plane_kernel,
        in_specs=[VMEM] * (1 + len(after)),
        out_specs=[VMEM, VMEM],
        out_shape=[jax.ShapeDtypeStruct(own.shape, jnp.float32), jax.ShapeDtypeStruct((planes, part, nz), jnp.float32)],
        compiler_params=params(2),
        name="plane_sums",
    )(own, *after)


def nearer_kernel(sums_ref, within_ref, *refs):
    back_ref = refs[-1]
    plane = lax.axis_index("z")
    total = jnp.zeros_like(sums_ref[0])
    for k in range(sums_ref.shape[0] - 1):
        total = total + sums_ref[k] * (k < plane).astype(jnp.float32)
    for k in range(within_ref.shape[0]):
        back_ref[k] = within_ref[k] + total


def nearer_of(sums, within, after):
    return pl.pallas_call(
        nearer_kernel,
        in_specs=[VMEM] * (2 + len(after)),
        out_specs=VMEM,
        out_shape=jax.ShapeDtypeStruct(within.shape, jnp.float32),
        compiler_params=params(2),
        name="nearer",
    )(sums, within, *after)


def brick_kernel(nx, ny, table_ref, d_ref, sent_ref, kept_ref, view_ref, done_ref, s_ref):
    own = lax.axis_index("depth")
    rows = nx // 2
    wide = 32
    done_ref[...] = jnp.zeros_like(done_ref)

    def along_x(part, _):
        carry = jnp.zeros((wide, LANES), jnp.float32)
        for x in range(nx):
            at = pl.ds(pl.multiple_of(x * ny + part * wide, 8), wide)
            cell = d_ref[at, :]
            s_ref[at, :] = carry + 0.5 * cell
            carry = carry + cell
        return 0

    lax.fori_loop(0, ny // wide, along_x, 0)
    view_rate = [factor(table_ref, c, 0) for c in range(3)]
    sun_rate = [factor(table_ref, c, 1) for c in range(3)]
    for out_ref, half in ((sent_ref, 1 - own), (kept_ref, own)):
        start = half * rows

        def cells(step, state, out_ref=out_ref, start=start):
            view, passing = list(state[0]), [list(p) for p in state[1]]
            for k in range(8):
                y = step * 8 + k
                light = [[None, None] for _ in range(3)]
                for t in range(2):
                    at = pl.ds((start + 8 * t) * ny + y, 8, stride=ny)
                    view[t] = view[t] + d_ref[at, :]
                    sun = s_ref[at, :]
                    for c in range(3):
                        later = jnp.exp2(view[t] * view_rate[c])
                        light[c][t] = (passing[c][t] - later) * jnp.exp2(sun * sun_rate[c])
                        passing[c][t] = later
                for c in range(3):
                    out_ref[0, c, y] = jnp.concatenate(light[c], axis=0).astype(out_ref.dtype)
            return tuple(view), tuple(tuple(p) for p in passing)

        zero, one = jnp.zeros((8, LANES), jnp.float32), jnp.ones((8, LANES), jnp.float32)
        view, _ = lax.fori_loop(0, ny // 8, cells, ((zero, zero), ((one, one),) * 3))
        for t in range(2):
            view_ref[pl.ds(pl.multiple_of(start + 8 * t, 8), 8), :] = view[t]


def brick_light_of(density, table, piece, after):
    nx, ny, nz = density.shape
    tiles = nz // LANES // PIECES
    light = pltpu.HBM((tiles, 3, ny, nx // 2, LANES), jnp.bfloat16)
    spec = pl.BlockSpec((1, 3, ny, nx // 2, LANES), lambda i: (i, 0, 0, 0, 0))
    ignore = len(after)

    def kernel(table_ref, d_ref, *refs):
        brick_kernel(nx, ny, table_ref, d_ref, *refs[ignore:])

    return pl.pallas_call(
        kernel,
        grid=(tiles,),
        in_specs=[VMEM, pl.BlockSpec((nx * ny, LANES), lambda i: (0, piece * tiles + i)), *[HBM] * ignore],
        out_specs=[spec, spec, pl.BlockSpec((nx, LANES), lambda i: (0, i)), VMEM],
        out_shape=[
            light,
            light,
            jax.ShapeDtypeStruct((nx, tiles * LANES), jnp.float32),
            jax.ShapeDtypeStruct((8, LANES), jnp.float32),
        ],
        scratch_shapes=[pltpu.VMEM((nx * ny, LANES), jnp.float32)],
        compiler_params=params(8),
        cost_estimate=cost(2**24, 2**23, 3 * 2**20),
        name=f"brick_light_{piece}",
    )(table, *in_hbm(density.reshape(nx * ny, nz), *after))


def sky_kernel(table_ref, *refs):
    passed_ref, behind_ref, front_ref = refs[-3:]
    views, others = refs[:PIECES], refs[PIECES : 2 * PIECES]
    _, rows, nz = passed_ref.shape
    own = lax.axis_index("depth")
    far = own.astype(jnp.float32)
    for lane in range(0, nz, LANES):
        piece, inner = divmod(lane, nz // PIECES)
        lanes, at = slice(lane, lane + LANES), slice(inner, inner + LANES)
        for row in range(0, rows, 8):
            mine = pl.ds(pl.multiple_of(own * rows + row, 8), 8)
            column = views[piece][mine, at] + others[piece][mine, at]
            for c in range(3):
                passed = jnp.exp2(column * factor(table_ref, c, 0))
                passed_ref[c, row : row + 8, lanes] = passed
                behind_ref[c, row : row + 8, lanes] = factor(table_ref, c, 3) * passed
        for j, half in enumerate((1 - own, own)):
            for row in range(0, rows, 8):
                mine = pl.ds(pl.multiple_of(half * rows + row, 8), 8)
                for c in range(3):
                    front_ref[j, c, row : row + 8, lanes] = jnp.exp2(others[piece][mine, at] * far * factor(table_ref, c, 0))


def sky_of(table, views, others):
    nx, width = views[0].shape
    shape = jax.ShapeDtypeStruct((3, nx // 2, width * PIECES), jnp.float32)
    return pl.pallas_call(
        sky_kernel,
        in_specs=[VMEM] * (1 + 2 * PIECES),
        out_specs=[VMEM, VMEM, VMEM],
        out_shape=[shape, shape, jax.ShapeDtypeStruct((2, *shape.shape), jnp.float32)],
        compiler_params=params(4),
        cost_estimate=cost(2**17, 2**20, 2**17),
        name="sky",
    )(table, *views, *others)


def pixel_kernel(own, table_ref, before_ref, front_ref, *refs):
    lights, start_ref, out_ref, a_ref, held_ref, sems = refs[:PIECES], refs[PIECES:-4], refs[-4], refs[-3], refs[-2], refs[-1]
    tiles, _, ny, rows, _ = lights[0].shape
    copies = [
        pltpu.make_async_copy(lights[piece].at[t, c], held_ref.at[piece * tiles + t, c], sems.at[piece * tiles + t, c])
        for piece in range(PIECES)
        for t in range(tiles)
        for c in range(3)
    ]
    for copy in copies:
        copy.start()
    for c in range(3):
        rate, colour = factor(table_ref, c, 1)[:1], factor(table_ref, c, 2)[:1]
        for t in range(tiles * PIECES):
            lanes = slice(t * LANES, (t + 1) * LANES)
            a_ref[c, :, lanes] = colour * jnp.exp2(before_ref[:, lanes] * rate)
    ways = 4
    for t in range(tiles * PIECES):
        lanes = slice(t * LANES, (t + 1) * LANES)
        for c in range(3):
            copies[3 * t + c].wait()
            total = [jnp.zeros((rows, LANES), jnp.float32) for _ in range(ways)]
            for y in range(ny):
                light = jnp.broadcast_to(a_ref[c, y : y + 1, lanes], (rows, LANES))
                total[y % ways] = total[y % ways] + light * held_ref[t, c, y].astype(jnp.float32)
            value = ((total[0] + total[1]) + (total[2] + total[3])) * front_ref[int(own), c, :, lanes]
            out_ref[c, :, lanes] = value + start_ref[0][c, :, lanes] if start_ref else value


def pixels_of(own, lights, before, front, table, name, *start):
    tiles, _, ny, rows, _ = lights[0].shape
    ny, nz = before.shape
    return pl.pallas_call(
        functools.partial(pixel_kernel, own),
        in_specs=[VMEM] * 3 + [HBM] * PIECES + [VMEM] * len(start),
        out_specs=VMEM,
        out_shape=jax.ShapeDtypeStruct((3, rows, nz), jnp.float32),
        scratch_shapes=[
            pltpu.VMEM((3, ny, nz), jnp.float32),
            pltpu.VMEM((tiles * PIECES, 3, ny, rows, LANES), jnp.bfloat16),
            pltpu.SemaphoreType.DMA((tiles * PIECES, 3)),
        ],
        compiler_params=params(8),
        cost_estimate=cost(2**21, 2**22, 2**16),
        name=name,
    )(table, before, front, *in_hbm(*lights), *start)


def per_device(sizes, density, extinction, sun_colour, sky_colour):
    planes, members, full_x, full_y = sizes
    nx, ny, nz = density.shape
    part = ny // members
    swap = functools.partial(lax.ppermute, axis_name="depth", perm=[(0, 1), (1, 0)])
    deal = functools.partial(lax.all_to_all, split_axis=0, concat_axis=0, tiled=True)
    column_light, table = load_of(density, extinction, sun_colour, sky_colour, full_x, full_y)
    own = deal(column_light.reshape(members, part, nz), PLANE)
    sent0, kept0, view0, done0 = brick_light_of(density, table, 0, ())
    within, sums = plane_of(own, planes, (done0,))
    sums = deal(sums, "z")
    sent1, kept1, view1, done1 = brick_light_of(density, table, 1, ())
    back = nearer_of(sums, within, (done1,))
    before = deal(back, PLANE).reshape(ny, nz)
    views = (view0, view1)
    transmittance, background, front = sky_of(table, views, [swap(view) for view in views])
    sent = pixels_of(False, (sent0, sent1), before, front, table, "pixels_sent")
    received = swap(sent)
    kept = pixels_of(True, (kept0, kept1), before, front, table, "pixels_kept", background)
    return kept + received, transmittance


def solution(mesh):
    shape = (8, 4, 2, 2, 2)
    fine = Mesh(mesh.devices.reshape(shape), ("z", *PLANE, "depth", "tile"))
    light = ("z", *PLANE)
    sizes = (8, 8, 2048, 128)
    return jax.shard_map(
        functools.partial(per_device, sizes),
        mesh=fine,
        in_specs=(P(light, "depth", "tile"), P(), P(), P()),
        out_specs=(P(None, (*light, "depth"), "tile"), P(None, (*light, "depth"), "tile")),
        check_vma=False,
    )
```

```python
import functools

import jax
import jax.numpy as jnp
from jax import lax
from jax.experimental import pallas as pl
from jax.experimental.pallas import tpu as pltpu
from jax.sharding import Mesh
from jax.sharding import PartitionSpec as P

LANES = 128
CHUNKS = 8
STEP = 8
WIDE = 32
LOG2E = 1.4426950408889634
VMEM = pl.BlockSpec(memory_space=pltpu.VMEM)
HBM = pl.BlockSpec(memory_space=pltpu.HBM)
PLANE = ("y", "x")


def params(mib):
    return pltpu.CompilerParams(vmem_limit_bytes=mib * 1024 * 1024)


def cost(flops, size, transcendentals=0):
    return pl.CostEstimate(flops=flops, bytes_accessed=size, transcendentals=transcendentals)


def in_hbm(*arrays):
    return [pltpu.with_memory_space_constraint(x, pltpu.HBM) for x in arrays]


def load_kernel(sizes, density_ref, ext_ref, sun_ref, sky_ref, light_ref, table_ref, held_ref, local_ref, three_ref, sems, small_sems):
    nx, ny, full_x, full_y = sizes
    tiles = held_ref.shape[0]
    planes = nx // CHUNKS
    copies = [
        [
            pltpu.make_async_copy(
                density_ref.at[pl.ds(k * planes, planes), :, pl.ds(t * LANES, LANES)],
                held_ref.at[t, pl.ds(k * planes, planes), pl.ds(0, ny)],
                sems.at[k, t],
            )
            for t in range(tiles)
        ]
        for k in range(CHUNKS)
    ]
    small = [
        pltpu.make_async_copy(source, three_ref.at[i], small_sems.at[i]) for i, source in enumerate((ext_ref, sun_ref, sky_ref))
    ]
    for chunk in copies:
        for copy in chunk:
            copy.start()
    for copy in small:
        copy.start()
    for k in range(CHUNKS):
        for t in range(tiles):
            copies[k][t].wait()
            lanes = slice(t * LANES, (t + 1) * LANES)
            for part in range(0, ny, WIDE):
                at = slice(part, part + WIDE)
                total = light_ref[at, lanes] if k else jnp.zeros((WIDE, LANES), jnp.float32)
                for x in range(k * planes, (k + 1) * planes):
                    cell = held_ref[t, x, at]
                    local_ref[t, x, at] = total + 0.5 * cell
                    total = total + cell
                light_ref[at, lanes] = total
    for copy in small:
        copy.wait()
    for c in range(3):
        row = (-LOG2E / full_y * three_ref[0, c], -LOG2E / full_x * three_ref[0, c], three_ref[1, c], three_ref[2, c])
        for i, value in enumerate(row):
            table_ref[8 * (4 * c + i) : 8 * (4 * c + i) + 8] = jnp.full((8, LANES), value, jnp.float32)


def factor(table_ref, c, which):
    return table_ref[8 * (4 * c + which) : 8 * (4 * c + which) + 8]


def load_of(density, extinction, sun_colour, sky_colour, full_x, full_y):
    nx, ny, nz = density.shape
    tiles = nz // LANES
    held = jax.ShapeDtypeStruct((tiles, nx, ny + 8, LANES), jnp.float32)
    return pl.pallas_call(
        functools.partial(load_kernel, (nx, ny, full_x, full_y)),
        in_specs=[HBM, HBM, HBM, HBM],
        out_specs=[VMEM, VMEM, VMEM, VMEM],
        out_shape=[
            jax.ShapeDtypeStruct((ny, nz), jnp.float32),
            jax.ShapeDtypeStruct((12 * 8, LANES), jnp.float32),
            held,
            held,
        ],
        scratch_shapes=[
            pltpu.SMEM((3, 3), jnp.float32),
            pltpu.SemaphoreType.DMA((CHUNKS, tiles)),
            pltpu.SemaphoreType.DMA((3,)),
        ],
        compiler_params=params(4),
        cost_estimate=cost(2**21, 2**23),
        name="load",
    )(*in_hbm(density, extinction, sun_colour, sky_colour))


def plane_kernel(own_ref, within_ref, sums_ref):
    total = jnp.zeros_like(own_ref[0])
    for k in range(own_ref.shape[0]):
        within_ref[k] = total
        total = total + own_ref[k]
    for k in range(sums_ref.shape[0]):
        sums_ref[k] = total


def plane_of(own, planes):
    _, part, nz = own.shape
    return pl.pallas_call(
        plane_kernel,
        in_specs=[VMEM],
        out_specs=[VMEM, VMEM],
        out_shape=[jax.ShapeDtypeStruct(own.shape, jnp.float32), jax.ShapeDtypeStruct((planes, part, nz), jnp.float32)],
        compiler_params=params(2),
        name="plane_sums",
    )(own)


def nearer_kernel(sums_ref, within_ref, back_ref):
    plane = lax.axis_index("z")
    total = jnp.zeros_like(sums_ref[0])
    for k in range(sums_ref.shape[0] - 1):
        total = total + sums_ref[k] * (k < plane).astype(jnp.float32)
    for k in range(within_ref.shape[0]):
        back_ref[k] = within_ref[k] + total


def nearer_of(sums, within):
    return pl.pallas_call(
        nearer_kernel,
        in_specs=[VMEM, VMEM],
        out_specs=VMEM,
        out_shape=jax.ShapeDtypeStruct(within.shape, jnp.float32),
        compiler_params=params(2),
        name="nearer",
    )(sums, within)


def pixel_kernel(own, sizes, table_ref, before_ref, held_ref, local_ref, out_ref, a_ref):
    nx, ny = sizes
    pitch = ny + 8
    tiles, _, _ = held_ref.shape
    rows = nx // 2
    for c in range(3):
        rate, colour = factor(table_ref, c, 1)[:1], factor(table_ref, c, 2)[:1]
        for t in range(tiles):
            a_ref[c, t] = colour * jnp.exp2(before_ref[:, t * LANES : (t + 1) * LANES] * rate)
    half = lax.axis_index("depth")
    start = (half if own else 1 - half) * rows
    view_rate = [factor(table_ref, c, 0) for c in range(3)]
    sun_rate = [factor(table_ref, c, 1) for c in range(3)]
    zero, one = jnp.zeros((8, LANES), jnp.float32), jnp.ones((8, LANES), jnp.float32)
    for tile in range(tiles):

        def cells(step, state, tile=tile):
            view = list(state[0])
            passing, total = ([list(p) for p in q] for q in state[1:])
            for k in range(STEP):
                y = step * STEP + k
                light = [jnp.broadcast_to(a_ref[c, tile, pl.ds(y, 1), :], (8, LANES)) for c in range(3)]
                for t in range(2):
                    at = pl.ds((start + 8 * t) * pitch + y, 8, stride=pitch)
                    view[t] = view[t] + held_ref[tile, at, :]
                    sun = local_ref[tile, at, :]
                    for c in range(3):
                        later = jnp.exp2(view[t] * view_rate[c])
                        total[c][t] = total[c][t] + (passing[c][t] - later) * (jnp.exp2(sun * sun_rate[c]) * light[c])
                        passing[c][t] = later
            return tuple(view), *(tuple(tuple(p) for p in q) for q in (passing, total))

        view, _, total = lax.fori_loop(0, ny // STEP, cells, ((zero, zero), ((one, one),) * 3, ((zero, zero),) * 3))
        lanes = slice(tile * LANES, (tile + 1) * LANES)
        for t in range(2):
            for c in range(3):
                out_ref[c, 8 * t : 8 * t + 8, lanes] = total[c][t]
            out_ref[3, 8 * t : 8 * t + 8, lanes] = view[t]


def pixels_of(own, before, table, held, local, name):
    ny, nz = before.shape
    tiles, nx, pitch, _ = held.shape
    flat = (tiles, nx * pitch, LANES)
    return pl.pallas_call(
        functools.partial(pixel_kernel, own, (nx, ny)),
        in_specs=[VMEM] * 4,
        out_specs=VMEM,
        out_shape=jax.ShapeDtypeStruct((4, nx // 2, nz), jnp.float32),
        scratch_shapes=[pltpu.VMEM((3, tiles, ny, LANES), jnp.float32)],
        compiler_params=params(4),
        cost_estimate=cost(2**24, 2**22, 2**21),
        name=name,
    )(table, before, held.reshape(flat), local.reshape(flat))


def image_kernel(table_ref, kept_ref, received_ref, image_ref, passed_ref):
    _, rows, nz = image_ref.shape
    near = lax.axis_index("depth") == 0
    for row in range(0, rows, 8):
        for lane in range(0, nz, LANES):
            at = (slice(row, row + 8), slice(lane, lane + LANES))
            mine, other = kept_ref[(3, *at)], received_ref[(3, *at)]
            front = jnp.where(near, mine, other)
            behind = jnp.where(near, other, mine)
            for c in range(3):
                rate = factor(table_ref, c, 0)
                passing = jnp.exp2(front * rate)
                passed = jnp.exp2((front + behind) * rate)
                mine_c, other_c = kept_ref[(c, *at)], received_ref[(c, *at)]
                near_c, far_c = jnp.where(near, mine_c, other_c), jnp.where(near, other_c, mine_c)
                passed_ref[(c, *at)] = passed
                image_ref[(c, *at)] = near_c + passing * far_c + factor(table_ref, c, 3) * passed


def image_of(table, kept, received):
    _, rows, nz = kept.shape
    shape = jax.ShapeDtypeStruct((3, rows, nz), jnp.float32)
    return pl.pallas_call(
        image_kernel,
        in_specs=[VMEM] * 3,
        out_specs=[VMEM, VMEM],
        out_shape=[shape, shape],
        compiler_params=params(4),
        name="image",
    )(table, kept, received)


def per_device(sizes, density, extinction, sun_colour, sky_colour):
    planes, members, full_x, full_y = sizes
    _, ny, nz = density.shape
    deal = functools.partial(lax.all_to_all, split_axis=0, concat_axis=0, tiled=True)
    column_light, table, held, local = load_of(density, extinction, sun_colour, sky_colour, full_x, full_y)
    within, sums = plane_of(deal(column_light.reshape(members, ny // members, nz), PLANE), planes)
    before = deal(nearer_of(deal(sums, "z"), within), PLANE).reshape(ny, nz)
    sent = pixels_of(False, before, table, held, local, "pixels_sent")
    received = lax.ppermute(sent, "depth", [(0, 1), (1, 0)])
    kept = pixels_of(True, before, table, held, local, "pixels_kept")
    return image_of(table, kept, received)


def solution(mesh):
    shape = (8, 4, 2, 2, 2)
    fine = Mesh(mesh.devices.reshape(shape), ("z", *PLANE, "depth", "tile"))
    light = ("z", *PLANE)
    sizes = (8, 8, 2048, 128)
    return jax.shard_map(
        functools.partial(per_device, sizes),
        mesh=fine,
        in_specs=(P(light, "depth", "tile"), P(), P(), P()),
        out_specs=(P(None, (*light, "depth"), "tile"), P(None, (*light, "depth"), "tile")),
        check_vma=False,
    )
```

```python
import functools

import jax
import jax.numpy as jnp
from jax import lax
from jax.experimental import pallas as pl
from jax.experimental.pallas import tpu as pltpu
from jax.sharding import Mesh
from jax.sharding import PartitionSpec as P

LANES = 128
CHUNKS = 8
STEP = 8
WIDE = 32
LOG2E = 1.4426950408889634
VMEM = pl.BlockSpec(memory_space=pltpu.VMEM)
HBM = pl.BlockSpec(memory_space=pltpu.HBM)


def params(mib):
    return pltpu.CompilerParams(vmem_limit_bytes=mib * 1024 * 1024)


def cost(flops, size, transcendentals=0):
    return pl.CostEstimate(flops=flops, bytes_accessed=size, transcendentals=transcendentals)


def in_hbm(*arrays):
    return [pltpu.with_memory_space_constraint(x, pltpu.HBM) for x in arrays]


def load_kernel(sizes, density_ref, ext_ref, sun_ref, sky_ref, light_ref, table_ref, held_ref, local_ref, sums_ref, three_ref, sems, small_sems):
    nx, ny, full_x, full_y = sizes
    tiles = held_ref.shape[0]
    planes = nx // CHUNKS
    copies = [
        [
            pltpu.make_async_copy(
                density_ref.at[pl.ds(k * planes, planes), :, pl.ds(t * LANES, LANES)],
                held_ref.at[t, pl.ds(k * planes, planes), pl.ds(0, ny)],
                sems.at[k, t],
            )
            for t in range(tiles)
        ]
        for k in range(CHUNKS)
    ]
    small = [
        pltpu.make_async_copy(source, three_ref.at[i], small_sems.at[i]) for i, source in enumerate((ext_ref, sun_ref, sky_ref))
    ]
    for chunk in copies:
        for copy in chunk:
            copy.start()
    for copy in small:
        copy.start()
    for k in range(CHUNKS):
        for t in range(tiles):
            copies[k][t].wait()
            for part in range(0, ny, WIDE):
                at = slice(part, part + WIDE)
                total = sums_ref[t, at] if k else jnp.zeros((WIDE, LANES), jnp.float32)
                for x in range(k * planes, (k + 1) * planes):
                    cell = held_ref[t, x, at]
                    local_ref[t, x, at] = total + 0.5 * cell
                    total = total + cell
                sums_ref[t, at] = total
    for t in range(tiles):
        light_ref[pl.ds(t, ny, stride=tiles), :] = sums_ref[t]
    for copy in small:
        copy.wait()
    for c in range(3):
        row = (-LOG2E / full_y * three_ref[0, c], -LOG2E / full_x * three_ref[0, c], three_ref[1, c], three_ref[2, c])
        for i, value in enumerate(row):
            table_ref[8 * (4 * c + i) : 8 * (4 * c + i) + 8] = jnp.full((8, LANES), value, jnp.float32)


def factor(table_ref, c, which):
    return table_ref[8 * (4 * c + which) : 8 * (4 * c + which) + 8]


def load_of(density, extinction, sun_colour, sky_colour, full_x, full_y):
    nx, ny, nz = density.shape
    tiles = nz // LANES
    held = jax.ShapeDtypeStruct((tiles, nx, ny + 8, LANES), jnp.float32)
    return pl.pallas_call(
        functools.partial(load_kernel, (nx, ny, full_x, full_y)),
        in_specs=[HBM, HBM, HBM, HBM],
        out_specs=[VMEM, VMEM, VMEM, VMEM],
        out_shape=[
            jax.ShapeDtypeStruct((ny * tiles, LANES), jnp.float32),
            jax.ShapeDtypeStruct((12 * 8, LANES), jnp.float32),
            held,
            held,
        ],
        scratch_shapes=[
            pltpu.VMEM((tiles, ny, LANES), jnp.float32),
            pltpu.SMEM((3, 3), jnp.float32),
            pltpu.SemaphoreType.DMA((CHUNKS, tiles)),
            pltpu.SemaphoreType.DMA((3,)),
        ],
        compiler_params=params(4),
        cost_estimate=cost(2**21, 2**23),
        name="load",
    )(*in_hbm(density, extinction, sun_colour, sky_colour))


def before_kernel(own_ref, dealt_ref):
    near = (lax.axis_index("x") == 0).astype(jnp.float32)
    total = jnp.zeros_like(own_ref[0])
    for k in range(own_ref.shape[0]):
        own = own_ref[k]
        dealt_ref[2 * k] = total
        dealt_ref[2 * k + 1] = total + near * own
        total = total + own


def before_of(own):
    pairs, rows, lanes = own.shape
    return pl.pallas_call(
        before_kernel,
        in_specs=[VMEM],
        out_specs=VMEM,
        out_shape=jax.ShapeDtypeStruct((2 * pairs, rows, lanes), jnp.float32),
        compiler_params=params(2),
        name="before",
    )(own)


def pixel_kernel(own, sizes, table_ref, before_ref, held_ref, local_ref, out_ref, a_ref):
    nx, ny = sizes
    pitch = ny + 8
    tiles, _, _ = held_ref.shape
    rows = nx // 2
    for c in range(3):
        rate, colour = factor(table_ref, c, 1), factor(table_ref, c, 2)
        for k in range(before_ref.shape[0] // 2):
            a_ref[c, 8 * k : 8 * k + 8] = colour * jnp.exp2((before_ref[2 * k] + before_ref[2 * k + 1]) * rate)
    half = lax.axis_index("depth")
    start = (half if own else 1 - half) * rows
    view_rate = [factor(table_ref, c, 0) for c in range(3)]
    sun_rate = [factor(table_ref, c, 1) for c in range(3)]
    zero, one = jnp.zeros((8, LANES), jnp.float32), jnp.ones((8, LANES), jnp.float32)
    for tile in range(tiles):

        def cells(step, state, tile=tile):
            view = list(state[0])
            passing, total = ([list(p) for p in q] for q in state[1:])
            for k in range(STEP):
                y = step * STEP + k
                light = [jnp.broadcast_to(a_ref[c, pl.ds(y * tiles + tile, 1), :], (8, LANES)) for c in range(3)]
                for t in range(2):
                    at = pl.ds((start + 8 * t) * pitch + y, 8, stride=pitch)
                    view[t] = view[t] + held_ref[tile, at, :]
                    sun = local_ref[tile, at, :]
                    for c in range(3):
                        later = jnp.exp2(view[t] * view_rate[c])
                        total[c][t] = total[c][t] + (passing[c][t] - later) * (jnp.exp2(sun * sun_rate[c]) * light[c])
                        passing[c][t] = later
            return tuple(view), *(tuple(tuple(p) for p in q) for q in (passing, total))

        view, _, total = lax.fori_loop(0, ny // STEP, cells, ((zero, zero), ((one, one),) * 3, ((zero, zero),) * 3))
        lanes = slice(tile * LANES, (tile + 1) * LANES)
        for t in range(2):
            for c in range(3):
                out_ref[c, 8 * t : 8 * t + 8, lanes] = total[c][t]
            out_ref[3, 8 * t : 8 * t + 8, lanes] = view[t]


def pixels_of(own, before, table, held, local, name):
    tiles, nx, pitch, _ = held.shape
    ny, nz = pitch - 8, tiles * LANES
    flat = (tiles, nx * pitch, LANES)
    return pl.pallas_call(
        functools.partial(pixel_kernel, own, (nx, ny)),
        in_specs=[VMEM] * 4,
        out_specs=VMEM,
        out_shape=jax.ShapeDtypeStruct((4, nx // 2, nz), jnp.float32),
        scratch_shapes=[pltpu.VMEM((3, ny * tiles, LANES), jnp.float32)],
        compiler_params=params(4),
        cost_estimate=cost(2**24, 2**22, 2**21),
        name=name,
    )(table, before, held.reshape(flat), local.reshape(flat))


def image_kernel(table_ref, kept_ref, received_ref, image_ref, passed_ref):
    _, rows, nz = image_ref.shape
    near = lax.axis_index("depth") == 0
    for row in range(0, rows, 8):
        for lane in range(0, nz, LANES):
            at = (slice(row, row + 8), slice(lane, lane + LANES))
            mine, other = kept_ref[(3, *at)], received_ref[(3, *at)]
            front = jnp.where(near, mine, other)
            behind = jnp.where(near, other, mine)
            for c in range(3):
                rate = factor(table_ref, c, 0)
                passing = jnp.exp2(front * rate)
                passed = jnp.exp2((front + behind) * rate)
                mine_c, other_c = kept_ref[(c, *at)], received_ref[(c, *at)]
                near_c, far_c = jnp.where(near, mine_c, other_c), jnp.where(near, other_c, mine_c)
                passed_ref[(c, *at)] = passed
                image_ref[(c, *at)] = near_c + passing * far_c + factor(table_ref, c, 3) * passed


def image_of(table, kept, received):
    _, rows, nz = kept.shape
    shape = jax.ShapeDtypeStruct((3, rows, nz), jnp.float32)
    return pl.pallas_call(
        image_kernel,
        in_specs=[VMEM] * 3,
        out_specs=[VMEM, VMEM],
        out_shape=[shape, shape],
        compiler_params=params(4),
        name="image",
    )(table, kept, received)


def per_device(sizes, density, extinction, sun_colour, sky_colour):
    pairs, full_x, full_y = sizes
    deal = functools.partial(lax.all_to_all, split_axis=0, concat_axis=0, tiled=True)
    column_light, table, held, local = load_of(density, extinction, sun_colour, sky_colour, full_x, full_y)
    own = deal(column_light.reshape(pairs, -1, LANES), ("z", "y"))
    before = deal(before_of(own), ("z", "y", "x"))
    sent = pixels_of(False, before, table, held, local, "pixels_sent")
    received = lax.ppermute(sent, "depth", [(0, 1), (1, 0)])
    kept = pixels_of(True, before, table, held, local, "pixels_kept")
    return image_of(table, kept, received)


def solution(mesh):
    shape = (8, 4, 2, 2, 2)
    light = ("z", "y", "x")
    fine = Mesh(mesh.devices.reshape(shape), (*light, "depth", "tile"))
    sizes = (32, 2048, 128)
    return jax.shard_map(
        functools.partial(per_device, sizes),
        mesh=fine,
        in_specs=(P(light, "depth", "tile"), P(), P(), P()),
        out_specs=(P(None, (*light, "depth"), "tile"), P(None, (*light, "depth"), "tile")),
        check_vma=False,
    )
```

```python
import functools

import jax
import jax.numpy as jnp
from jax import lax
from jax.experimental import pallas as pl
from jax.experimental.pallas import tpu as pltpu
from jax.sharding import Mesh
from jax.sharding import PartitionSpec as P

LANES = 128
CHUNKS = 8
STEP = 8
PITCH = 72
AHEAD = 3
WIDE = 32
LOG2E = 1.4426950408889634
VMEM = pl.BlockSpec(memory_space=pltpu.VMEM)
HBM = pl.BlockSpec(memory_space=pltpu.HBM)


def params(mib):
    return pltpu.CompilerParams(vmem_limit_bytes=mib * 1024 * 1024)


def cost(flops, size, transcendentals=0):
    return pl.CostEstimate(flops=flops, bytes_accessed=size, transcendentals=transcendentals)


def in_hbm(*arrays):
    return [pltpu.with_memory_space_constraint(x, pltpu.HBM) for x in arrays]


def load_kernel(sizes, density_ref, ext_ref, sun_ref, sky_ref, light_ref, table_ref, held_ref, local_ref, view_ref, ready_ref, sums_ref, three_ref, sems, small_sems):
    nx, ny, full_x, full_y = sizes
    tiles = held_ref.shape[0]
    planes = nx // CHUNKS
    copies = [
        [
            pltpu.make_async_copy(
                density_ref.at[pl.ds(k * planes, planes), :, pl.ds(t * LANES, LANES)],
                held_ref.at[t, pl.ds(k * planes, planes), pl.ds(0, ny)],
                sems.at[k, t],
            )
            for t in range(tiles)
        ]
        for k in range(CHUNKS)
    ]
    small = [
        pltpu.make_async_copy(source, three_ref.at[i], small_sems.at[i]) for i, source in enumerate((ext_ref, sun_ref, sky_ref))
    ]
    for chunk in copies:
        for copy in chunk:
            copy.start()
    for copy in small:
        copy.start()
    for k in range(CHUNKS):
        for t in range(tiles):
            copies[k][t].wait()
            for part in range(0, ny, WIDE):
                at = slice(part, part + WIDE)
                total = sums_ref[t, at] if k else jnp.zeros((WIDE, LANES), jnp.float32)
                for x in range(k * planes, (k + 1) * planes):
                    cell = held_ref[t, x, at]
                    local_ref[t, x, at] = total + 0.5 * cell
                    total = total + cell
                sums_ref[t, at] = total
    for t in range(tiles):
        light_ref[pl.ds(t, ny, stride=tiles), :] = sums_ref[t]
    for copy in small:
        copy.wait()
    for c in range(3):
        row = (-LOG2E / full_y * three_ref[0, c], -LOG2E / full_x * three_ref[0, c], three_ref[1, c], three_ref[2, c])
        for i, value in enumerate(row):
            table_ref[8 * (4 * c + i) : 8 * (4 * c + i) + 8] = jnp.full((8, LANES), value, jnp.float32)

    @pl.when(lax.axis_index("z") < AHEAD)
    def _():
        flat = (nx * PITCH, LANES)
        for t in range(tiles):
            held, local = held_ref.at[t].reshape(*flat), local_ref.at[t].reshape(*flat)
            for start in range(0, nx, 16):

                def keep(y, i, c, light, t=t, start=start):
                    ready_ref[t, c, pl.ds((start + 8 * i) * PITCH + y, 8, stride=PITCH), :] = light

                view, _ = march(table_ref, held, local, start, ny, keep)
                for i in range(2):
                    view_ref[start + 8 * i : start + 8 * i + 8, t * LANES : (t + 1) * LANES] = view[i]


def march(table_ref, held_ref, local_ref, start, ny, use, state=()):
    view_rate = [factor(table_ref, c, 0) for c in range(3)]
    sun_rate = [factor(table_ref, c, 1) for c in range(3)]
    zero, one = jnp.zeros((8, LANES), jnp.float32), jnp.ones((8, LANES), jnp.float32)

    def cells(step, carry):
        view, passing, state = list(carry[0]), [list(p) for p in carry[1]], carry[2]
        for k in range(STEP):
            y = step * STEP + k
            for i in range(2):
                at = pl.ds((start + 8 * i) * PITCH + y, 8, stride=PITCH)
                view[i] = view[i] + held_ref[at, :]
                sun = local_ref[at, :]
                for c in range(3):
                    later = jnp.exp2(view[i] * view_rate[c])
                    light = (passing[c][i] - later) * jnp.exp2(sun * sun_rate[c])
                    passing[c][i] = later
                    if state:
                        state = use(y, i, c, light, state)
                    else:
                        use(y, i, c, light)
        return tuple(view), tuple(tuple(p) for p in passing), state

    view, _, state = lax.fori_loop(0, ny // STEP, cells, ((zero, zero), ((one, one),) * 3, state))
    return view, state


def factor(table_ref, c, which):
    return table_ref[8 * (4 * c + which) : 8 * (4 * c + which) + 8]


def load_of(density, extinction, sun_colour, sky_colour, full_x, full_y):
    nx, ny, nz = density.shape
    tiles = nz // LANES
    held = jax.ShapeDtypeStruct((tiles, nx, PITCH, LANES), jnp.float32)
    return pl.pallas_call(
        functools.partial(load_kernel, (nx, ny, full_x, full_y)),
        in_specs=[HBM, HBM, HBM, HBM],
        out_specs=[VMEM] * 6,
        out_shape=[
            jax.ShapeDtypeStruct((ny * tiles, LANES), jnp.float32),
            jax.ShapeDtypeStruct((12 * 8, LANES), jnp.float32),
            held,
            held,
            jax.ShapeDtypeStruct((nx, nz), jnp.float32),
            jax.ShapeDtypeStruct((tiles, 3, nx * PITCH, LANES), jnp.float32),
        ],
        scratch_shapes=[
            pltpu.VMEM((tiles, ny, LANES), jnp.float32),
            pltpu.SMEM((3, 3), jnp.float32),
            pltpu.SemaphoreType.DMA((CHUNKS, tiles)),
            pltpu.SemaphoreType.DMA((3,)),
        ],
        compiler_params=params(4),
        cost_estimate=cost(2**21, 2**23),
        name="load",
    )(*in_hbm(density, extinction, sun_colour, sky_colour))


def before_kernel(own_ref, dealt_ref):
    near = (lax.axis_index("x") == 0).astype(jnp.float32)
    total = jnp.zeros_like(own_ref[0])
    for k in range(own_ref.shape[0]):
        own = own_ref[k]
        dealt_ref[2 * k] = total
        dealt_ref[2 * k + 1] = total + near * own
        total = total + own


def before_of(own):
    pairs, rows, lanes = own.shape
    return pl.pallas_call(
        before_kernel,
        in_specs=[VMEM],
        out_specs=VMEM,
        out_shape=jax.ShapeDtypeStruct((2 * pairs, rows, lanes), jnp.float32),
        compiler_params=params(2),
        name="before",
    )(own)


def pixel_kernel(own, sizes, table_ref, before_ref, held_ref, local_ref, view_ref, ready_ref, out_ref, a_ref):
    nx, ny = sizes
    tiles, _, _ = held_ref.shape
    rows = nx // 2
    for c in range(3):
        rate, colour = factor(table_ref, c, 1), factor(table_ref, c, 2)
        for k in range(before_ref.shape[0] // 2):
            a_ref[c, 8 * k : 8 * k + 8] = colour * jnp.exp2((before_ref[2 * k] + before_ref[2 * k + 1]) * rate)
    half = lax.axis_index("depth")
    start = (half if own else 1 - half) * rows
    ahead = lax.axis_index("z") < AHEAD

    @pl.when(ahead)
    def _():
        out_ref[3] = view_ref[pl.ds(pl.multiple_of(start, 8), rows), :]
        for t in range(tiles):
            for c in range(3):
                light = a_ref[c, pl.ds(t, ny, stride=tiles), :].reshape(ny // 8, 8, LANES)
                for row in range(0, rows, 8):
                    parts = []
                    for x in range(8):
                        at = pl.ds(pl.multiple_of((start + row + x) * PITCH, 8), ny)
                        cells = ready_ref[t, c, at, :].reshape(ny // 8, 8, LANES)
                        parts.append(jnp.sum(light * cells, axis=0))
                    out_ref[c, row : row + 8, t * LANES : (t + 1) * LANES] = jnp.sum(jnp.stack(parts), axis=1)

    @pl.when(jnp.logical_not(ahead))
    def _():
        for t in range(tiles):

            def add(y, i, c, light, total, t=t):
                total = [list(q) for q in total]
                total[c][i] = total[c][i] + light * jnp.broadcast_to(a_ref[c, pl.ds(y * tiles + t, 1), :], (8, LANES))
                return tuple(tuple(q) for q in total)

            zero = jnp.zeros((8, LANES), jnp.float32)
            view, total = march(table_ref, held_ref.at[t], local_ref.at[t], start, ny, add, ((zero, zero),) * 3)
            lanes = slice(t * LANES, (t + 1) * LANES)
            for i in range(2):
                for c in range(3):
                    out_ref[c, 8 * i : 8 * i + 8, lanes] = total[c][i]
                out_ref[3, 8 * i : 8 * i + 8, lanes] = view[i]


def pixels_of(own, before, table, held, local, view, ready, name):
    tiles, nx, _, _ = held.shape
    ny, nz = before.size // (2 * tiles * LANES), tiles * LANES
    flat = (tiles, nx * PITCH, LANES)
    return pl.pallas_call(
        functools.partial(pixel_kernel, own, (nx, ny)),
        in_specs=[VMEM] * 6,
        out_specs=VMEM,
        out_shape=jax.ShapeDtypeStruct((4, nx // 2, nz), jnp.float32),
        scratch_shapes=[pltpu.VMEM((3, ny * tiles, LANES), jnp.float32)],
        compiler_params=params(4),
        cost_estimate=cost(2**24, 2**22, 2**21),
        name=name,
    )(table, before, held.reshape(flat), local.reshape(flat), view, ready)


def image_kernel(table_ref, kept_ref, received_ref, image_ref, passed_ref):
    _, rows, nz = image_ref.shape
    near = lax.axis_index("depth") == 0
    for row in range(0, rows, 8):
        for lane in range(0, nz, LANES):
            at = (slice(row, row + 8), slice(lane, lane + LANES))
            mine, other = kept_ref[(3, *at)], received_ref[(3, *at)]
            front = jnp.where(near, mine, other)
            behind = jnp.where(near, other, mine)
            for c in range(3):
                rate = factor(table_ref, c, 0)
                passing = jnp.exp2(front * rate)
                passed = jnp.exp2((front + behind) * rate)
                mine_c, other_c = kept_ref[(c, *at)], received_ref[(c, *at)]
                near_c, far_c = jnp.where(near, mine_c, other_c), jnp.where(near, other_c, mine_c)
                passed_ref[(c, *at)] = passed
                image_ref[(c, *at)] = near_c + passing * far_c + factor(table_ref, c, 3) * passed


def image_of(table, kept, received):
    _, rows, nz = kept.shape
    shape = jax.ShapeDtypeStruct((3, rows, nz), jnp.float32)
    return pl.pallas_call(
        image_kernel,
        in_specs=[VMEM] * 3,
        out_specs=[VMEM, VMEM],
        out_shape=[shape, shape],
        compiler_params=params(4),
        name="image",
    )(table, kept, received)


def per_device(sizes, density, extinction, sun_colour, sky_colour):
    pairs, full_x, full_y = sizes
    deal = functools.partial(lax.all_to_all, split_axis=0, concat_axis=0, tiled=True)
    column_light, table, *brick = load_of(density, extinction, sun_colour, sky_colour, full_x, full_y)
    own = deal(column_light.reshape(pairs, -1, LANES), ("z", "y"))
    before = deal(before_of(own), ("z", "y", "x"))
    sent = pixels_of(False, before, table, *brick, "pixels_sent")
    received = lax.ppermute(sent, "depth", [(0, 1), (1, 0)])
    kept = pixels_of(True, before, table, *brick, "pixels_kept")
    return image_of(table, kept, received)


def solution(mesh):
    shape = (8, 4, 2, 2, 2)
    light = ("z", "y", "x")
    fine = Mesh(mesh.devices.reshape(shape), (*light, "depth", "tile"))
    sizes = (32, 2048, 128)
    return jax.shard_map(
        functools.partial(per_device, sizes),
        mesh=fine,
        in_specs=(P(light, "depth", "tile"), P(), P(), P()),
        out_specs=(P(None, (*light, "depth"), "tile"), P(None, (*light, "depth"), "tile")),
        check_vma=False,
    )
```

```python
import functools

import jax
import jax.numpy as jnp
from jax import lax
from jax.experimental import pallas as pl
from jax.experimental.pallas import tpu as pltpu
from jax.sharding import Mesh
from jax.sharding import PartitionSpec as P

LANES = 128
CHUNKS = 4
STEP = 8
PITCH = 72
WIDE = 32
LOG2E = 1.4426950408889634
VMEM = pl.BlockSpec(memory_space=pltpu.VMEM)
HBM = pl.BlockSpec(memory_space=pltpu.HBM)


def params(mib):
    return pltpu.CompilerParams(vmem_limit_bytes=mib * 1024 * 1024)


def cost(flops, size, transcendentals=0):
    return pl.CostEstimate(flops=flops, bytes_accessed=size, transcendentals=transcendentals)


def in_hbm(*arrays):
    return [pltpu.with_memory_space_constraint(x, pltpu.HBM) for x in arrays]


def works_ahead():
    z, y, x, tile = (lax.axis_index(axis) for axis in ("z", "y", "x", "tile"))
    late = jnp.where(z < 4, 13 * z, 75 - 4 * z) + 9 * jnp.minimum(y, 2) + jnp.where(x == 0, 5 * tile, 21)
    return late <= 55


def load_kernel(sizes, density_ref, ext_ref, sun_ref, sky_ref, light_ref, table_ref, held_ref, local_ref, view_ref, ready_ref, sums_ref, columns_ref, three_ref, sems, small_sems):
    nx, ny, full_x, full_y = sizes
    tiles = held_ref.shape[0]
    planes = nx // CHUNKS
    copies = [
        [
            pltpu.make_async_copy(
                density_ref.at[pl.ds(k * planes, planes), :, pl.ds(t * LANES, LANES)],
                held_ref.at[t, pl.ds(k * planes, planes), pl.ds(0, ny)],
                sems.at[k, t],
            )
            for t in range(tiles)
        ]
        for k in range(CHUNKS)
    ]
    small = [
        pltpu.make_async_copy(source, three_ref.at[i], small_sems.at[i]) for i, source in enumerate((ext_ref, sun_ref, sky_ref))
    ]
    for chunk in copies:
        for copy in chunk:
            copy.start()
    for copy in small:
        copy.start()
    for k in range(CHUNKS):
        for t in range(tiles):
            copies[k][t].wait()
            for part in range(0, ny, WIDE):
                at = slice(part, part + WIDE)
                total = sums_ref[t, at] if k else jnp.zeros((WIDE, LANES), jnp.float32)
                for x in range(k * planes, (k + 1) * planes):
                    cell = held_ref[t, x, at]
                    local_ref[t, x, at] = total + 0.5 * cell
                    total = total + cell
                sums_ref[t, at] = total
    for t in range(tiles):
        columns_ref[pl.ds(t, ny, stride=tiles), :] = sums_ref[t]
    for k in range(light_ref.shape[0]):
        light_ref[k] = columns_ref[8 * (k // 2) : 8 * (k // 2) + 8]
    for copy in small:
        copy.wait()
    for c in range(3):
        row = (-LOG2E / full_y * three_ref[0, c], -LOG2E / full_x * three_ref[0, c], three_ref[1, c], three_ref[2, c])
        for i, value in enumerate(row):
            table_ref[8 * (4 * c + i) : 8 * (4 * c + i) + 8] = jnp.full((8, LANES), value, jnp.float32)

    @pl.when(works_ahead())
    def _():
        flat = (nx * PITCH, LANES)
        for t in range(tiles):
            held, local = held_ref.at[t].reshape(*flat), local_ref.at[t].reshape(*flat)
            for start in range(0, nx, 16):

                def keep(y, i, c, light, t=t, start=start):
                    ready_ref[t, c, pl.ds((start + 8 * i) * PITCH + y, 8, stride=PITCH), :] = light

                view, _ = march(table_ref, held, local, start, ny, keep)
                for i in range(2):
                    view_ref[start + 8 * i : start + 8 * i + 8, t * LANES : (t + 1) * LANES] = view[i]


def march(table_ref, held_ref, local_ref, start, ny, use, state=()):
    view_rate = [factor(table_ref, c, 0) for c in range(3)]
    sun_rate = [factor(table_ref, c, 1) for c in range(3)]
    zero, one = jnp.zeros((8, LANES), jnp.float32), jnp.ones((8, LANES), jnp.float32)

    def cells(step, carry):
        view, passing, state = list(carry[0]), [list(p) for p in carry[1]], carry[2]
        for k in range(STEP):
            y = step * STEP + k
            for i in range(2):
                at = pl.ds((start + 8 * i) * PITCH + y, 8, stride=PITCH)
                view[i] = view[i] + held_ref[at, :]
                sun = local_ref[at, :]
                for c in range(3):
                    later = jnp.exp2(view[i] * view_rate[c])
                    light = (passing[c][i] - later) * jnp.exp2(sun * sun_rate[c])
                    passing[c][i] = later
                    if state:
                        state = use(y, i, c, light, state)
                    else:
                        use(y, i, c, light)
        return tuple(view), tuple(tuple(p) for p in passing), state

    view, _, state = lax.fori_loop(0, ny // STEP, cells, ((zero, zero), ((one, one),) * 3, state))
    return view, state


def factor(table_ref, c, which):
    return table_ref[8 * (4 * c + which) : 8 * (4 * c + which) + 8]


def load_of(density, extinction, sun_colour, sky_colour, full_x, full_y):
    nx, ny, nz = density.shape
    tiles = nz // LANES
    held = jax.ShapeDtypeStruct((tiles, nx, PITCH, LANES), jnp.float32)
    return pl.pallas_call(
        functools.partial(load_kernel, (nx, ny, full_x, full_y)),
        in_specs=[HBM, HBM, HBM, HBM],
        out_specs=[VMEM] * 6,
        out_shape=[
            jax.ShapeDtypeStruct((ny * tiles // 4, 8, LANES), jnp.float32),
            jax.ShapeDtypeStruct((12 * 8, LANES), jnp.float32),
            held,
            held,
            jax.ShapeDtypeStruct((nx, nz), jnp.float32),
            jax.ShapeDtypeStruct((tiles, 3, nx * PITCH, LANES), jnp.float32),
        ],
        scratch_shapes=[
            pltpu.VMEM((tiles, ny, LANES), jnp.float32),
            pltpu.VMEM((ny * tiles, LANES), jnp.float32),
            pltpu.SMEM((3, 3), jnp.float32),
            pltpu.SemaphoreType.DMA((CHUNKS, tiles)),
            pltpu.SemaphoreType.DMA((3,)),
        ],
        compiler_params=params(4),
        cost_estimate=cost(2**21, 2**23),
        name="load",
    )(*in_hbm(density, extinction, sun_colour, sky_colour))


def before_kernel(own_ref, dealt_ref):
    far = (lax.axis_index("x") == 1).astype(jnp.float32)
    total = jnp.zeros_like(own_ref[0])
    for k in range(dealt_ref.shape[0]):
        near = own_ref[2 * k]
        dealt_ref[k] = total + far * near
        total = total + (near + own_ref[2 * k + 1])


def before_of(own):
    count, rows, lanes = own.shape
    return pl.pallas_call(
        before_kernel,
        in_specs=[VMEM],
        out_specs=VMEM,
        out_shape=jax.ShapeDtypeStruct((count // 2, rows, lanes), jnp.float32),
        compiler_params=params(2),
        name="before",
    )(own)


def pixel_kernel(own, sizes, table_ref, before_ref, held_ref, local_ref, view_ref, ready_ref, out_ref, a_ref):
    nx, ny = sizes
    tiles, _, _ = held_ref.shape
    rows = nx // 2
    for c in range(3):
        rate, colour = factor(table_ref, c, 1), factor(table_ref, c, 2)
        for k in range(before_ref.shape[0]):
            a_ref[c, 8 * k : 8 * k + 8] = colour * jnp.exp2(before_ref[k] * rate)
    half = lax.axis_index("depth")
    start = (half if own else 1 - half) * rows
    ahead = works_ahead()

    @pl.when(ahead)
    def _():
        out_ref[3] = view_ref[pl.ds(pl.multiple_of(start, 8), rows), :]
        for t in range(tiles):
            for c in range(3):
                light = a_ref[c, pl.ds(t, ny, stride=tiles), :].reshape(ny // 8, 8, LANES)
                for row in range(0, rows, 8):
                    parts = []
                    for x in range(8):
                        at = pl.ds(pl.multiple_of((start + row + x) * PITCH, 8), ny)
                        cells = ready_ref[t, c, at, :].reshape(ny // 8, 8, LANES)
                        parts.append(jnp.sum(light * cells, axis=0))
                    out_ref[c, row : row + 8, t * LANES : (t + 1) * LANES] = jnp.sum(jnp.stack(parts), axis=1)

    @pl.when(jnp.logical_not(ahead))
    def _():
        for t in range(tiles):

            def add(y, i, c, light, total, t=t):
                total = [list(q) for q in total]
                total[c][i] = total[c][i] + light * jnp.broadcast_to(a_ref[c, pl.ds(y * tiles + t, 1), :], (8, LANES))
                return tuple(tuple(q) for q in total)

            zero = jnp.zeros((8, LANES), jnp.float32)
            view, total = march(table_ref, held_ref.at[t], local_ref.at[t], start, ny, add, ((zero, zero),) * 3)
            lanes = slice(t * LANES, (t + 1) * LANES)
            for i in range(2):
                for c in range(3):
                    out_ref[c, 8 * i : 8 * i + 8, lanes] = total[c][i]
                out_ref[3, 8 * i : 8 * i + 8, lanes] = view[i]


def pixels_of(own, before, table, held, local, view, ready, name):
    tiles, nx, _, _ = held.shape
    ny, nz = before.size // (tiles * LANES), tiles * LANES
    flat = (tiles, nx * PITCH, LANES)
    return pl.pallas_call(
        functools.partial(pixel_kernel, own, (nx, ny)),
        in_specs=[VMEM] * 6,
        out_specs=VMEM,
        out_shape=jax.ShapeDtypeStruct((4, nx // 2, nz), jnp.float32),
        scratch_shapes=[pltpu.VMEM((3, ny * tiles, LANES), jnp.float32)],
        compiler_params=params(4),
        cost_estimate=cost(2**24, 2**22, 2**21),
        name=name,
    )(table, before, held.reshape(flat), local.reshape(flat), view, ready)


def image_kernel(table_ref, kept_ref, received_ref, image_ref, passed_ref):
    _, rows, nz = image_ref.shape
    near = lax.axis_index("depth") == 0
    for row in range(0, rows, 8):
        for lane in range(0, nz, LANES):
            at = (slice(row, row + 8), slice(lane, lane + LANES))
            mine, other = kept_ref[(3, *at)], received_ref[(3, *at)]
            front = jnp.where(near, mine, other)
            behind = jnp.where(near, other, mine)
            for c in range(3):
                rate = factor(table_ref, c, 0)
                passing = jnp.exp2(front * rate)
                passed = jnp.exp2((front + behind) * rate)
                mine_c, other_c = kept_ref[(c, *at)], received_ref[(c, *at)]
                near_c, far_c = jnp.where(near, mine_c, other_c), jnp.where(near, other_c, mine_c)
                passed_ref[(c, *at)] = passed
                image_ref[(c, *at)] = near_c + passing * far_c + factor(table_ref, c, 3) * passed


def image_of(table, kept, received):
    _, rows, nz = kept.shape
    shape = jax.ShapeDtypeStruct((3, rows, nz), jnp.float32)
    return pl.pallas_call(
        image_kernel,
        in_specs=[VMEM] * 3,
        out_specs=[VMEM, VMEM],
        out_shape=[shape, shape],
        compiler_params=params(4),
        name="image",
    )(table, kept, received)


def per_device(sizes, density, extinction, sun_colour, sky_colour):
    full_x, full_y = sizes
    deal = functools.partial(lax.all_to_all, split_axis=0, concat_axis=0, tiled=True)
    column_light, table, *brick = load_of(density, extinction, sun_colour, sky_colour, full_x, full_y)
    before = deal(before_of(deal(column_light, ("z", "y", "x"))), ("z", "y"))
    sent = pixels_of(False, before, table, *brick, "pixels_sent")
    received = lax.ppermute(sent, "depth", [(0, 1), (1, 0)])
    kept = pixels_of(True, before, table, *brick, "pixels_kept")
    return image_of(table, kept, received)


def solution(mesh):
    shape = (8, 4, 2, 2, 2)
    light = ("z", "y", "x")
    fine = Mesh(mesh.devices.reshape(shape), (*light, "depth", "tile"))
    sizes = (2048, 128)
    return jax.shard_map(
        functools.partial(per_device, sizes),
        mesh=fine,
        in_specs=(P(light, "depth", "tile"), P(), P(), P()),
        out_specs=(P(None, (*light, "depth"), "tile"), P(None, (*light, "depth"), "tile")),
        check_vma=False,
    )
```

```python
import functools

import jax
import jax.numpy as jnp
from jax import lax
from jax.experimental import pallas as pl
from jax.experimental.pallas import tpu as pltpu
from jax.sharding import Mesh
from jax.sharding import PartitionSpec as P

LANES = 128
CHUNKS = 4
STEP = 8
PITCH = 72
WIDE = 32
LOG2E = 1.4426950408889634
VMEM = pl.BlockSpec(memory_space=pltpu.VMEM)
HBM = pl.BlockSpec(memory_space=pltpu.HBM)


def params(mib):
    return pltpu.CompilerParams(vmem_limit_bytes=mib * 1024 * 1024)


def cost(flops, size, transcendentals=0):
    return pl.CostEstimate(flops=flops, bytes_accessed=size, transcendentals=transcendentals)


def in_hbm(*arrays):
    return [pltpu.with_memory_space_constraint(x, pltpu.HBM) for x in arrays]


def works_ahead():
    z, y, x, tile = (lax.axis_index(axis) for axis in ("z", "y", "x", "tile"))
    late = jnp.where(z < 4, 13 * z, 75 - 4 * z) + 9 * jnp.minimum(y, 2) + jnp.where(x == 0, 5 * tile, 21)
    return late <= 55


def load_kernel(sizes, density_ref, ext_ref, sun_ref, sky_ref, light_ref, table_ref, held_ref, local_ref, view_ref, ready_ref, sums_ref, three_ref, sems, small_sems):
    nx, ny, full_x, full_y = sizes
    tiles = held_ref.shape[0]
    planes = nx // CHUNKS
    copies = [
        [
            pltpu.make_async_copy(
                density_ref.at[pl.ds(k * planes, planes), :, pl.ds(t * LANES, LANES)],
                held_ref.at[t, pl.ds(k * planes, planes), pl.ds(0, ny)],
                sems.at[k, t],
            )
            for t in range(tiles)
        ]
        for k in range(CHUNKS)
    ]
    small = [
        pltpu.make_async_copy(source, three_ref.at[i], small_sems.at[i]) for i, source in enumerate((ext_ref, sun_ref, sky_ref))
    ]
    for chunk in copies:
        for copy in chunk:
            copy.start()
    for copy in small:
        copy.start()
    for k in range(CHUNKS):
        for t in range(tiles):
            copies[k][t].wait()
            for part in range(0, ny, WIDE):
                at = slice(part, part + WIDE)
                total = sums_ref[t, at] if k else jnp.zeros((WIDE, LANES), jnp.float32)
                for x in range(k * planes, (k + 1) * planes):
                    cell = held_ref[t, x, at]
                    local_ref[t, x, at] = total + 0.5 * cell
                    total = total + cell
                sums_ref[t, at] = total
    for t in range(tiles):
        light_ref[pl.ds(t, ny, stride=tiles), :] = sums_ref[t]
    for copy in small:
        copy.wait()
    for c in range(3):
        row = (-LOG2E / full_y * three_ref[0, c], -LOG2E / full_x * three_ref[0, c], three_ref[1, c], three_ref[2, c])
        for i, value in enumerate(row):
            table_ref[8 * (4 * c + i) : 8 * (4 * c + i) + 8] = jnp.full((8, LANES), value, jnp.float32)

    @pl.when(works_ahead())
    def _():
        flat = (nx * PITCH, LANES)
        for t in range(tiles):
            held, local = held_ref.at[t].reshape(*flat), local_ref.at[t].reshape(*flat)
            for start in range(0, nx, 16):

                def keep(y, i, c, light, t=t, start=start):
                    ready_ref[t, c, pl.ds((start + 8 * i) * PITCH + y, 8, stride=PITCH), :] = light

                view, _ = march(table_ref, held, local, start, ny, keep)
                for i in range(2):
                    view_ref[start + 8 * i : start + 8 * i + 8, t * LANES : (t + 1) * LANES] = view[i]


def march(table_ref, held_ref, local_ref, start, ny, use, state=()):
    view_rate = [factor(table_ref, c, 0) for c in range(3)]
    sun_rate = [factor(table_ref, c, 1) for c in range(3)]
    zero, one = jnp.zeros((8, LANES), jnp.float32), jnp.ones((8, LANES), jnp.float32)

    def cells(step, carry):
        view, passing, state = list(carry[0]), [list(p) for p in carry[1]], carry[2]
        for k in range(STEP):
            y = step * STEP + k
            for i in range(2):
                at = pl.ds((start + 8 * i) * PITCH + y, 8, stride=PITCH)
                view[i] = view[i] + held_ref[at, :]
                sun = local_ref[at, :]
                for c in range(3):
                    later = jnp.exp2(view[i] * view_rate[c])
                    light = (passing[c][i] - later) * jnp.exp2(sun * sun_rate[c])
                    passing[c][i] = later
                    if state:
                        state = use(y, i, c, light, state)
                    else:
                        use(y, i, c, light)
        return tuple(view), tuple(tuple(p) for p in passing), state

    view, _, state = lax.fori_loop(0, ny // STEP, cells, ((zero, zero), ((one, one),) * 3, state))
    return view, state


def factor(table_ref, c, which):
    return table_ref[8 * (4 * c + which) : 8 * (4 * c + which) + 8]


def load_of(density, extinction, sun_colour, sky_colour, full_x, full_y):
    nx, ny, nz = density.shape
    tiles = nz // LANES
    held = jax.ShapeDtypeStruct((tiles, nx, PITCH, LANES), jnp.float32)
    return pl.pallas_call(
        functools.partial(load_kernel, (nx, ny, full_x, full_y)),
        in_specs=[HBM, HBM, HBM, HBM],
        out_specs=[VMEM] * 6,
        out_shape=[
            jax.ShapeDtypeStruct((ny * tiles, LANES), jnp.float32),
            jax.ShapeDtypeStruct((12 * 8, LANES), jnp.float32),
            held,
            held,
            jax.ShapeDtypeStruct((nx, nz), jnp.float32),
            jax.ShapeDtypeStruct((tiles, 3, nx * PITCH, LANES), jnp.float32),
        ],
        scratch_shapes=[
            pltpu.VMEM((tiles, ny, LANES), jnp.float32),
            pltpu.SMEM((3, 3), jnp.float32),
            pltpu.SemaphoreType.DMA((CHUNKS, tiles)),
            pltpu.SemaphoreType.DMA((3,)),
        ],
        compiler_params=params(4),
        cost_estimate=cost(2**21, 2**23),
        name="load",
    )(*in_hbm(density, extinction, sun_colour, sky_colour))


def before_kernel(own_ref, dealt_ref):
    near = (lax.axis_index("x") == 0).astype(jnp.float32)
    total = jnp.zeros_like(own_ref[0])
    for k in range(own_ref.shape[0]):
        own = own_ref[k]
        dealt_ref[2 * k] = total
        dealt_ref[2 * k + 1] = total + near * own
        total = total + own


def before_of(own):
    pairs, rows, lanes = own.shape
    return pl.pallas_call(
        before_kernel,
        in_specs=[VMEM],
        out_specs=VMEM,
        out_shape=jax.ShapeDtypeStruct((2 * pairs, rows, lanes), jnp.float32),
        compiler_params=params(2),
        name="before",
    )(own)


def pixel_kernel(own, sizes, table_ref, before_ref, held_ref, local_ref, view_ref, ready_ref, out_ref, a_ref):
    nx, ny = sizes
    tiles, _, _ = held_ref.shape
    rows = nx // 2
    for c in range(3):
        rate, colour = factor(table_ref, c, 1), factor(table_ref, c, 2)
        for k in range(before_ref.shape[0] // 2):
            a_ref[c, 8 * k : 8 * k + 8] = colour * jnp.exp2((before_ref[2 * k] + before_ref[2 * k + 1]) * rate)
    half = lax.axis_index("depth")
    start = (half if own else 1 - half) * rows
    ahead = works_ahead()

    @pl.when(ahead)
    def _():
        out_ref[3] = view_ref[pl.ds(pl.multiple_of(start, 8), rows), :]
        for t in range(tiles):
            for c in range(3):
                light = a_ref[c, pl.ds(t, ny, stride=tiles), :].reshape(ny // 8, 8, LANES)
                for row in range(0, rows, 8):
                    parts = []
                    for x in range(8):
                        at = pl.ds(pl.multiple_of((start + row + x) * PITCH, 8), ny)
                        cells = ready_ref[t, c, at, :].reshape(ny // 8, 8, LANES)
                        parts.append(jnp.sum(light * cells, axis=0))
                    out_ref[c, row : row + 8, t * LANES : (t + 1) * LANES] = jnp.sum(jnp.stack(parts), axis=1)

    @pl.when(jnp.logical_not(ahead))
    def _():
        for t in range(tiles):

            def add(y, i, c, light, total, t=t):
                total = [list(q) for q in total]
                total[c][i] = total[c][i] + light * jnp.broadcast_to(a_ref[c, pl.ds(y * tiles + t, 1), :], (8, LANES))
                return tuple(tuple(q) for q in total)

            zero = jnp.zeros((8, LANES), jnp.float32)
            view, total = march(table_ref, held_ref.at[t], local_ref.at[t], start, ny, add, ((zero, zero),) * 3)
            lanes = slice(t * LANES, (t + 1) * LANES)
            for i in range(2):
                for c in range(3):
                    out_ref[c, 8 * i : 8 * i + 8, lanes] = total[c][i]
                out_ref[3, 8 * i : 8 * i + 8, lanes] = view[i]


def pixels_of(own, before, table, held, local, view, ready, name):
    tiles, nx, _, _ = held.shape
    ny, nz = before.size // (2 * tiles * LANES), tiles * LANES
    flat = (tiles, nx * PITCH, LANES)
    return pl.pallas_call(
        functools.partial(pixel_kernel, own, (nx, ny)),
        in_specs=[VMEM] * 6,
        out_specs=VMEM,
        out_shape=jax.ShapeDtypeStruct((4, nx // 2, nz), jnp.float32),
        scratch_shapes=[pltpu.VMEM((3, ny * tiles, LANES), jnp.float32)],
        compiler_params=params(4),
        cost_estimate=cost(2**24, 2**22, 2**21),
        name=name,
    )(table, before, held.reshape(flat), local.reshape(flat), view, ready)


def image_kernel(table_ref, kept_ref, received_ref, image_ref, passed_ref):
    _, rows, nz = image_ref.shape
    near = lax.axis_index("depth") == 0
    for row in range(0, rows, 8):
        for lane in range(0, nz, LANES):
            at = (slice(row, row + 8), slice(lane, lane + LANES))
            mine, other = kept_ref[(3, *at)], received_ref[(3, *at)]
            front = jnp.where(near, mine, other)
            behind = jnp.where(near, other, mine)
            for c in range(3):
                rate = factor(table_ref, c, 0)
                passing = jnp.exp2(front * rate)
                passed = jnp.exp2((front + behind) * rate)
                mine_c, other_c = kept_ref[(c, *at)], received_ref[(c, *at)]
                near_c, far_c = jnp.where(near, mine_c, other_c), jnp.where(near, other_c, mine_c)
                passed_ref[(c, *at)] = passed
                image_ref[(c, *at)] = near_c + passing * far_c + factor(table_ref, c, 3) * passed


def image_of(table, kept, received):
    _, rows, nz = kept.shape
    shape = jax.ShapeDtypeStruct((3, rows, nz), jnp.float32)
    return pl.pallas_call(
        image_kernel,
        in_specs=[VMEM] * 3,
        out_specs=[VMEM, VMEM],
        out_shape=[shape, shape],
        compiler_params=params(4),
        name="image",
    )(table, kept, received)


def per_device(sizes, density, extinction, sun_colour, sky_colour):
    full_x, full_y = sizes
    deal = functools.partial(lax.all_to_all, split_axis=0, concat_axis=0, tiled=True)
    column_light, table, *brick = load_of(density, extinction, sun_colour, sky_colour, full_x, full_y)
    own = deal(column_light.reshape(-1, 8, LANES), ("z", "y"))
    before = deal(before_of(own), ("z", "y", "x"))
    sent = pixels_of(False, before, table, *brick, "pixels_sent")
    received = lax.ppermute(sent, "depth", [(0, 1), (1, 0)])
    kept = pixels_of(True, before, table, *brick, "pixels_kept")
    return image_of(table, kept, received)


def solution(mesh):
    shape = (8, 4, 2, 2, 2)
    light = ("z", "y", "x")
    fine = Mesh(mesh.devices.reshape(shape), (*light, "depth", "tile"))
    sizes = (2048, 128)
    return jax.shard_map(
        functools.partial(per_device, sizes),
        mesh=fine,
        in_specs=(P(light, "depth", "tile"), P(), P(), P()),
        out_specs=(P(None, (*light, "depth"), "tile"), P(None, (*light, "depth"), "tile")),
        check_vma=False,
    )
```

```python
import functools

import jax
import jax.numpy as jnp
from jax import lax
from jax.experimental import pallas as pl
from jax.experimental.pallas import tpu as pltpu
from jax.sharding import Mesh
from jax.sharding import PartitionSpec as P

LANES = 128
CHUNKS = 4
STEP = 8
PITCH = 72
COLUMNS = 4
WIDE = 32
LOG2E = 1.4426950408889634
VMEM = pl.BlockSpec(memory_space=pltpu.VMEM)
HBM = pl.BlockSpec(memory_space=pltpu.HBM)


def params(mib):
    return pltpu.CompilerParams(vmem_limit_bytes=mib * 1024 * 1024)


def cost(flops, size, transcendentals=0):
    return pl.CostEstimate(flops=flops, bytes_accessed=size, transcendentals=transcendentals)


def in_hbm(*arrays):
    return [pltpu.with_memory_space_constraint(x, pltpu.HBM) for x in arrays]


def works_ahead():
    z, y, x, tile = (lax.axis_index(axis) for axis in ("z", "y", "x", "tile"))
    late = jnp.where(z < 4, 13 * z, 75 - 4 * z) + 9 * jnp.minimum(y, 2) + jnp.where(x == 0, 5 * tile, 21)
    return late <= 55


def load_kernel(sizes, density_ref, ext_ref, sun_ref, sky_ref, light_ref, table_ref, held_ref, local_ref, view_ref, ready_ref, sums_ref, three_ref, sems, small_sems):
    nx, ny, full_x, full_y = sizes
    tiles = held_ref.shape[0]
    planes = nx // CHUNKS
    copies = [
        [
            pltpu.make_async_copy(
                density_ref.at[pl.ds(k * planes, planes), :, pl.ds(t * LANES, LANES)],
                held_ref.at[t, pl.ds(k * planes, planes), pl.ds(0, ny)],
                sems.at[k, t],
            )
            for t in range(tiles)
        ]
        for k in range(CHUNKS)
    ]
    small = [
        pltpu.make_async_copy(source, three_ref.at[i], small_sems.at[i]) for i, source in enumerate((ext_ref, sun_ref, sky_ref))
    ]
    for chunk in copies:
        for copy in chunk:
            copy.start()
    for copy in small:
        copy.start()
    for k in range(CHUNKS):
        for t in range(tiles):
            copies[k][t].wait()
            for part in range(0, ny, WIDE):
                at = slice(part, part + WIDE)
                total = sums_ref[t, at] if k else jnp.zeros((WIDE, LANES), jnp.float32)
                for x in range(k * planes, (k + 1) * planes):
                    cell = held_ref[t, x, at]
                    local_ref[t, x, at] = total + 0.5 * cell
                    total = total + cell
                sums_ref[t, at] = total
    for t in range(tiles):
        light_ref[pl.ds(t, ny, stride=tiles), :] = sums_ref[t]
    for copy in small:
        copy.wait()
    for c in range(3):
        row = (-LOG2E / full_y * three_ref[0, c], -LOG2E / full_x * three_ref[0, c], three_ref[1, c], three_ref[2, c])
        for i, value in enumerate(row):
            table_ref[8 * (4 * c + i) : 8 * (4 * c + i) + 8] = jnp.full((8, LANES), value, jnp.float32)

    @pl.when(works_ahead())
    def _():
        flat = (nx * PITCH, LANES)
        for t in range(tiles):
            held, local = held_ref.at[t].reshape(*flat), local_ref.at[t].reshape(*flat)
            for start in range(0, nx, 16):

                def keep(y, i, c, light, t=t, start=start):
                    ready_ref[t, c, pl.ds((start + 8 * i) * PITCH + y, 8, stride=PITCH), :] = light

                view, _ = march(table_ref, held, local, start, ny, keep)
                for i in range(2):
                    view_ref[start + 8 * i : start + 8 * i + 8, t * LANES : (t + 1) * LANES] = view[i]


def march(table_ref, held_ref, local_ref, start, ny, use, state=()):
    view_rate = [factor(table_ref, c, 0) for c in range(3)]
    sun_rate = [factor(table_ref, c, 1) for c in range(3)]
    zero, one = jnp.zeros((8, LANES), jnp.float32), jnp.ones((8, LANES), jnp.float32)

    def cells(step, carry):
        view, passing, state = list(carry[0]), [list(p) for p in carry[1]], carry[2]
        for k in range(STEP):
            y = step * STEP + k
            for i in range(2):
                at = pl.ds((start + 8 * i) * PITCH + y, 8, stride=PITCH)
                view[i] = view[i] + held_ref[at, :]
                sun = local_ref[at, :]
                for c in range(3):
                    later = jnp.exp2(view[i] * view_rate[c])
                    light = (passing[c][i] - later) * jnp.exp2(sun * sun_rate[c])
                    passing[c][i] = later
                    if state:
                        state = use(y, i, c, light, state)
                    else:
                        use(y, i, c, light)
        return tuple(view), tuple(tuple(p) for p in passing), state

    view, _, state = lax.fori_loop(0, ny // STEP, cells, ((zero, zero), ((one, one),) * 3, state))
    return view, state


def factor(table_ref, c, which):
    return table_ref[8 * (4 * c + which) : 8 * (4 * c + which) + 8]


def load_of(density, extinction, sun_colour, sky_colour, full_x, full_y):
    nx, ny, nz = density.shape
    tiles = nz // LANES
    held = jax.ShapeDtypeStruct((tiles, nx, PITCH, LANES), jnp.float32)
    return pl.pallas_call(
        functools.partial(load_kernel, (nx, ny, full_x, full_y)),
        in_specs=[HBM, HBM, HBM, HBM],
        out_specs=[VMEM] * 6,
        out_shape=[
            jax.ShapeDtypeStruct((ny * tiles, LANES), jnp.float32),
            jax.ShapeDtypeStruct((12 * 8, LANES), jnp.float32),
            held,
            held,
            jax.ShapeDtypeStruct((nx, nz), jnp.float32),
            jax.ShapeDtypeStruct((tiles, 3, nx * PITCH, LANES), jnp.float32),
        ],
        scratch_shapes=[
            pltpu.VMEM((tiles, ny, LANES), jnp.float32),
            pltpu.SMEM((3, 3), jnp.float32),
            pltpu.SemaphoreType.DMA((CHUNKS, tiles)),
            pltpu.SemaphoreType.DMA((3,)),
        ],
        compiler_params=params(4),
        cost_estimate=cost(2**21, 2**23),
        name="load",
    )(*in_hbm(density, extinction, sun_colour, sky_colour))


def place(k, pairs):
    z, y = divmod(k, COLUMNS)
    return 2 * (y * (pairs // COLUMNS) + z)


def before_kernel(own_ref, dealt_ref):
    near = (lax.axis_index("x") == 0).astype(jnp.float32)
    total = jnp.zeros_like(own_ref[0])
    for k in range(own_ref.shape[0]):
        own = own_ref[k]
        at = place(k, own_ref.shape[0])
        dealt_ref[at] = total
        dealt_ref[at + 1] = total + near * own
        total = total + own


def before_of(own):
    pairs, rows, lanes = own.shape
    return pl.pallas_call(
        before_kernel,
        in_specs=[VMEM],
        out_specs=VMEM,
        out_shape=jax.ShapeDtypeStruct((2 * pairs, rows, lanes), jnp.float32),
        compiler_params=params(2),
        name="before",
    )(own)


def pixel_kernel(own, sizes, table_ref, before_ref, held_ref, local_ref, view_ref, ready_ref, out_ref, a_ref):
    nx, ny = sizes
    tiles, _, _ = held_ref.shape
    rows = nx // 2
    for c in range(3):
        rate, colour = factor(table_ref, c, 1), factor(table_ref, c, 2)
        for k in range(before_ref.shape[0] // 2):
            at = place(k, before_ref.shape[0] // 2)
            a_ref[c, 8 * k : 8 * k + 8] = colour * jnp.exp2((before_ref[at] + before_ref[at + 1]) * rate)
    half = lax.axis_index("depth")
    start = (half if own else 1 - half) * rows
    ahead = works_ahead()

    @pl.when(ahead)
    def _():
        out_ref[3] = view_ref[pl.ds(pl.multiple_of(start, 8), rows), :]
        for t in range(tiles):
            for c in range(3):
                light = a_ref[c, pl.ds(t, ny, stride=tiles), :].reshape(ny // 8, 8, LANES)
                for row in range(0, rows, 8):
                    parts = []
                    for x in range(8):
                        at = pl.ds(pl.multiple_of((start + row + x) * PITCH, 8), ny)
                        cells = ready_ref[t, c, at, :].reshape(ny // 8, 8, LANES)
                        parts.append(jnp.sum(light * cells, axis=0))
                    out_ref[c, row : row + 8, t * LANES : (t + 1) * LANES] = jnp.sum(jnp.stack(parts), axis=1)

    @pl.when(jnp.logical_not(ahead))
    def _():
        for t in range(tiles):

            def add(y, i, c, light, total, t=t):
                total = [list(q) for q in total]
                total[c][i] = total[c][i] + light * jnp.broadcast_to(a_ref[c, pl.ds(y * tiles + t, 1), :], (8, LANES))
                return tuple(tuple(q) for q in total)

            zero = jnp.zeros((8, LANES), jnp.float32)
            view, total = march(table_ref, held_ref.at[t], local_ref.at[t], start, ny, add, ((zero, zero),) * 3)
            lanes = slice(t * LANES, (t + 1) * LANES)
            for i in range(2):
                for c in range(3):
                    out_ref[c, 8 * i : 8 * i + 8, lanes] = total[c][i]
                out_ref[3, 8 * i : 8 * i + 8, lanes] = view[i]


def pixels_of(own, before, table, held, local, view, ready, name):
    tiles, nx, _, _ = held.shape
    ny, nz = before.size // (2 * tiles * LANES), tiles * LANES
    flat = (tiles, nx * PITCH, LANES)
    return pl.pallas_call(
        functools.partial(pixel_kernel, own, (nx, ny)),
        in_specs=[VMEM] * 6,
        out_specs=VMEM,
        out_shape=jax.ShapeDtypeStruct((4, nx // 2, nz), jnp.float32),
        scratch_shapes=[pltpu.VMEM((3, ny * tiles, LANES), jnp.float32)],
        compiler_params=params(4),
        cost_estimate=cost(2**24, 2**22, 2**21),
        name=name,
    )(table, before, held.reshape(flat), local.reshape(flat), view, ready)


def image_kernel(table_ref, kept_ref, received_ref, image_ref, passed_ref):
    _, rows, nz = image_ref.shape
    near = lax.axis_index("depth") == 0
    for row in range(0, rows, 8):
        for lane in range(0, nz, LANES):
            at = (slice(row, row + 8), slice(lane, lane + LANES))
            mine, other = kept_ref[(3, *at)], received_ref[(3, *at)]
            front = jnp.where(near, mine, other)
            behind = jnp.where(near, other, mine)
            for c in range(3):
                rate = factor(table_ref, c, 0)
                passing = jnp.exp2(front * rate)
                passed = jnp.exp2((front + behind) * rate)
                mine_c, other_c = kept_ref[(c, *at)], received_ref[(c, *at)]
                near_c, far_c = jnp.where(near, mine_c, other_c), jnp.where(near, other_c, mine_c)
                passed_ref[(c, *at)] = passed
                image_ref[(c, *at)] = near_c + passing * far_c + factor(table_ref, c, 3) * passed


def image_of(table, kept, received):
    _, rows, nz = kept.shape
    shape = jax.ShapeDtypeStruct((3, rows, nz), jnp.float32)
    return pl.pallas_call(
        image_kernel,
        in_specs=[VMEM] * 3,
        out_specs=[VMEM, VMEM],
        out_shape=[shape, shape],
        compiler_params=params(4),
        name="image",
    )(table, kept, received)


def per_device(sizes, density, extinction, sun_colour, sky_colour):
    full_x, full_y = sizes
    deal = functools.partial(lax.all_to_all, split_axis=0, concat_axis=0, tiled=True)
    column_light, table, *brick = load_of(density, extinction, sun_colour, sky_colour, full_x, full_y)
    own = deal(column_light.reshape(-1, 8, LANES), ("z", "y"))
    before = deal(before_of(own), ("y", "z", "x"))
    sent = pixels_of(False, before, table, *brick, "pixels_sent")
    received = lax.ppermute(sent, "depth", [(0, 1), (1, 0)])
    kept = pixels_of(True, before, table, *brick, "pixels_kept")
    return image_of(table, kept, received)


def solution(mesh):
    shape = (8, 4, 2, 2, 2)
    light = ("z", "y", "x")
    fine = Mesh(mesh.devices.reshape(shape), (*light, "depth", "tile"))
    sizes = (2048, 128)
    return jax.shard_map(
        functools.partial(per_device, sizes),
        mesh=fine,
        in_specs=(P(light, "depth", "tile"), P(), P(), P()),
        out_specs=(P(None, (*light, "depth"), "tile"), P(None, (*light, "depth"), "tile")),
        check_vma=False,
    )
```

```python
import functools

import jax
import jax.numpy as jnp
from jax import lax
from jax.experimental import pallas as pl
from jax.experimental.pallas import tpu as pltpu
from jax.sharding import PartitionSpec as P

LANES = 128
CHUNKS = 4
STEP = 8
PITCH = 72
COLUMNS = 4
WIDE = 32
LOG2E = 1.4426950408889634
VMEM = pl.BlockSpec(memory_space=pltpu.VMEM)
HBM = pl.BlockSpec(memory_space=pltpu.HBM)


def params(mib):
    return pltpu.CompilerParams(vmem_limit_bytes=mib * 1024 * 1024)


def cost(flops, size, transcendentals=0):
    return pl.CostEstimate(flops=flops, bytes_accessed=size, transcendentals=transcendentals)


def in_hbm(*arrays):
    return [pltpu.with_memory_space_constraint(x, pltpu.HBM) for x in arrays]


def light_place():
    light = lax.axis_index("light")
    return light // (2 * COLUMNS), light // 2 % COLUMNS, light % 2


def works_ahead():
    z, y, x = light_place()
    tile = lax.axis_index("tile")
    late = jnp.where(z < 4, 13 * z, 75 - 4 * z) + 9 * jnp.minimum(y, 2) + jnp.where(x == 0, 5 * tile, 21)
    return late <= 55


def load_kernel(sizes, density_ref, ext_ref, sun_ref, sky_ref, light_ref, table_ref, held_ref, local_ref, view_ref, ready_ref, sums_ref, three_ref, sems, small_sems):
    nx, ny, full_x, full_y = sizes
    tiles = held_ref.shape[0]
    planes = nx // CHUNKS
    copies = [
        [
            pltpu.make_async_copy(
                density_ref.at[pl.ds(k * planes, planes), :, pl.ds(t * LANES, LANES)],
                held_ref.at[t, pl.ds(k * planes, planes), pl.ds(0, ny)],
                sems.at[k, t],
            )
            for t in range(tiles)
        ]
        for k in range(CHUNKS)
    ]
    small = [
        pltpu.make_async_copy(source, three_ref.at[i], small_sems.at[i]) for i, source in enumerate((ext_ref, sun_ref, sky_ref))
    ]
    for chunk in copies:
        for copy in chunk:
            copy.start()
    for copy in small:
        copy.start()
    for k in range(CHUNKS):
        for t in range(tiles):
            copies[k][t].wait()
            for part in range(0, ny, WIDE):
                at = slice(part, part + WIDE)
                total = sums_ref[t, at] if k else jnp.zeros((WIDE, LANES), jnp.float32)
                for x in range(k * planes, (k + 1) * planes):
                    cell = held_ref[t, x, at]
                    local_ref[t, x, at] = total + 0.5 * cell
                    total = total + cell
                sums_ref[t, at] = total
    for t in range(tiles):
        light_ref[pl.ds(t, ny, stride=tiles), :] = sums_ref[t]
    for copy in small:
        copy.wait()
    for c in range(3):
        row = (-LOG2E / full_y * three_ref[0, c], -LOG2E / full_x * three_ref[0, c], three_ref[1, c], three_ref[2, c])
        for i, value in enumerate(row):
            table_ref[8 * (4 * c + i) : 8 * (4 * c + i) + 8] = jnp.full((8, LANES), value, jnp.float32)

    @pl.when(works_ahead())
    def _():
        flat = (nx * PITCH, LANES)
        for t in range(tiles):
            held, local = held_ref.at[t].reshape(*flat), local_ref.at[t].reshape(*flat)
            for start in range(0, nx, 16):

                def keep(y, i, c, light, t=t, start=start):
                    ready_ref[t, c, pl.ds((start + 8 * i) * PITCH + y, 8, stride=PITCH), :] = light

                view, _ = march(table_ref, held, local, start, ny, keep)
                for i in range(2):
                    view_ref[start + 8 * i : start + 8 * i + 8, t * LANES : (t + 1) * LANES] = view[i]


def march(table_ref, held_ref, local_ref, start, ny, use, state=()):
    view_rate = [factor(table_ref, c, 0) for c in range(3)]
    sun_rate = [factor(table_ref, c, 1) for c in range(3)]
    zero, one = jnp.zeros((8, LANES), jnp.float32), jnp.ones((8, LANES), jnp.float32)

    def cells(step, carry):
        view, passing, state = list(carry[0]), [list(p) for p in carry[1]], carry[2]
        for k in range(STEP):
            y = step * STEP + k
            for i in range(2):
                at = pl.ds((start + 8 * i) * PITCH + y, 8, stride=PITCH)
                view[i] = view[i] + held_ref[at, :]
                sun = local_ref[at, :]
                for c in range(3):
                    later = jnp.exp2(view[i] * view_rate[c])
                    light = (passing[c][i] - later) * jnp.exp2(sun * sun_rate[c])
                    passing[c][i] = later
                    if state:
                        state = use(y, i, c, light, state)
                    else:
                        use(y, i, c, light)
        return tuple(view), tuple(tuple(p) for p in passing), state

    view, _, state = lax.fori_loop(0, ny // STEP, cells, ((zero, zero), ((one, one),) * 3, state))
    return view, state


def factor(table_ref, c, which):
    return table_ref[8 * (4 * c + which) : 8 * (4 * c + which) + 8]


def load_of(density, extinction, sun_colour, sky_colour, full_x, full_y):
    nx, ny, nz = density.shape
    tiles = nz // LANES
    held = jax.ShapeDtypeStruct((tiles, nx, PITCH, LANES), jnp.float32)
    return pl.pallas_call(
        functools.partial(load_kernel, (nx, ny, full_x, full_y)),
        in_specs=[HBM, HBM, HBM, HBM],
        out_specs=[VMEM] * 6,
        out_shape=[
            jax.ShapeDtypeStruct((ny * tiles, LANES), jnp.float32),
            jax.ShapeDtypeStruct((12 * 8, LANES), jnp.float32),
            held,
            held,
            jax.ShapeDtypeStruct((nx, nz), jnp.float32),
            jax.ShapeDtypeStruct((tiles, 3, nx * PITCH, LANES), jnp.float32),
        ],
        scratch_shapes=[
            pltpu.VMEM((tiles, ny, LANES), jnp.float32),
            pltpu.SMEM((3, 3), jnp.float32),
            pltpu.SemaphoreType.DMA((CHUNKS, tiles)),
            pltpu.SemaphoreType.DMA((3,)),
        ],
        compiler_params=params(4),
        cost_estimate=cost(2**21, 2**23),
        name="load",
    )(*in_hbm(density, extinction, sun_colour, sky_colour))


def second_round():
    return sorted(range(64), key=lambda i: (i // 2 % COLUMNS, i // 8, i % 2))[::-1]


def place(k, x):
    return second_round().index(2 * k + x)


def before_kernel(own_ref, dealt_ref):
    near = (light_place()[2] == 0).astype(jnp.float32)
    total = jnp.zeros_like(own_ref[0])
    for k in range(own_ref.shape[0]):
        own = own_ref[own_ref.shape[0] - 1 - k]
        dealt_ref[place(k, 0)] = total
        dealt_ref[place(k, 1)] = total + near * own
        total = total + own


def before_of(own):
    pairs, rows, lanes = own.shape
    return pl.pallas_call(
        before_kernel,
        in_specs=[VMEM],
        out_specs=VMEM,
        out_shape=jax.ShapeDtypeStruct((2 * pairs, rows, lanes), jnp.float32),
        compiler_params=params(2),
        name="before",
    )(own)


def pixel_kernel(own, sizes, table_ref, before_ref, held_ref, local_ref, view_ref, ready_ref, out_ref, a_ref):
    nx, ny = sizes
    tiles, _, _ = held_ref.shape
    rows = nx // 2
    for c in range(3):
        rate, colour = factor(table_ref, c, 1), factor(table_ref, c, 2)
        for k in range(before_ref.shape[0] // 2):
            column = before_ref[place(k, 0)] + before_ref[place(k, 1)]
            row = 8 * (before_ref.shape[0] // 2 - 1 - k)
            a_ref[c, row : row + 8] = colour * jnp.exp2(column * rate)
    half = lax.axis_index("depth")
    start = (half if own else 1 - half) * rows
    ahead = works_ahead()

    @pl.when(ahead)
    def _():
        out_ref[3] = view_ref[pl.ds(pl.multiple_of(start, 8), rows), :]
        for t in range(tiles):
            for c in range(3):
                light = a_ref[c, pl.ds(t, ny, stride=tiles), :].reshape(ny // 8, 8, LANES)
                for row in range(0, rows, 8):
                    parts = []
                    for x in range(8):
                        at = pl.ds(pl.multiple_of((start + row + x) * PITCH, 8), ny)
                        cells = ready_ref[t, c, at, :].reshape(ny // 8, 8, LANES)
                        parts.append(jnp.sum(light * cells, axis=0))
                    out_ref[c, row : row + 8, t * LANES : (t + 1) * LANES] = jnp.sum(jnp.stack(parts), axis=1)

    @pl.when(jnp.logical_not(ahead))
    def _():
        for t in range(tiles):

            def add(y, i, c, light, total, t=t):
                total = [list(q) for q in total]
                total[c][i] = total[c][i] + light * jnp.broadcast_to(a_ref[c, pl.ds(y * tiles + t, 1), :], (8, LANES))
                return tuple(tuple(q) for q in total)

            zero = jnp.zeros((8, LANES), jnp.float32)
            view, total = march(table_ref, held_ref.at[t], local_ref.at[t], start, ny, add, ((zero, zero),) * 3)
            lanes = slice(t * LANES, (t + 1) * LANES)
            for i in range(2):
                for c in range(3):
                    out_ref[c, 8 * i : 8 * i + 8, lanes] = total[c][i]
                out_ref[3, 8 * i : 8 * i + 8, lanes] = view[i]


def pixels_of(own, before, table, held, local, view, ready, name):
    tiles, nx, _, _ = held.shape
    ny, nz = before.size // (2 * tiles * LANES), tiles * LANES
    flat = (tiles, nx * PITCH, LANES)
    return pl.pallas_call(
        functools.partial(pixel_kernel, own, (nx, ny)),
        in_specs=[VMEM] * 6,
        out_specs=VMEM,
        out_shape=jax.ShapeDtypeStruct((4, nx // 2, nz), jnp.float32),
        scratch_shapes=[pltpu.VMEM((3, ny * tiles, LANES), jnp.float32)],
        compiler_params=params(4),
        cost_estimate=cost(2**24, 2**22, 2**21),
        name=name,
    )(table, before, held.reshape(flat), local.reshape(flat), view, ready)


def image_kernel(table_ref, kept_ref, received_ref, image_ref, passed_ref):
    _, rows, nz = image_ref.shape
    near = lax.axis_index("depth") == 0
    for row in range(0, rows, 8):
        for lane in range(0, nz, LANES):
            at = (slice(row, row + 8), slice(lane, lane + LANES))
            mine, other = kept_ref[(3, *at)], received_ref[(3, *at)]
            front = jnp.where(near, mine, other)
            behind = jnp.where(near, other, mine)
            for c in range(3):
                rate = factor(table_ref, c, 0)
                passing = jnp.exp2(front * rate)
                passed = jnp.exp2((front + behind) * rate)
                mine_c, other_c = kept_ref[(c, *at)], received_ref[(c, *at)]
                near_c, far_c = jnp.where(near, mine_c, other_c), jnp.where(near, other_c, mine_c)
                passed_ref[(c, *at)] = passed
                image_ref[(c, *at)] = near_c + passing * far_c + factor(table_ref, c, 3) * passed


def image_of(table, kept, received):
    _, rows, nz = kept.shape
    shape = jax.ShapeDtypeStruct((3, rows, nz), jnp.float32)
    return pl.pallas_call(
        image_kernel,
        in_specs=[VMEM] * 3,
        out_specs=[VMEM, VMEM],
        out_shape=[shape, shape],
        compiler_params=params(4),
        name="image",
    )(table, kept, received)


def per_device(sizes, density, extinction, sun_colour, sky_colour):
    full_x, full_y = sizes
    deal = functools.partial(lax.all_to_all, axis_name="light", split_axis=0, concat_axis=0, tiled=True)
    column_light, table, *brick = load_of(density, extinction, sun_colour, sky_colour, full_x, full_y)
    count = lax.axis_size("light")
    own = deal(column_light.reshape(-1, 8, LANES), axis_index_groups=[list(range(x, count, 2))[::-1] for x in range(2)])
    before = deal(before_of(own), axis_index_groups=[second_round()])
    sent = pixels_of(False, before, table, *brick, "pixels_sent")
    received = lax.ppermute(sent, "depth", [(0, 1), (1, 0)])
    kept = pixels_of(True, before, table, *brick, "pixels_kept")
    return image_of(table, kept, received)


def solution(mesh):
    sizes = (2048, 128)
    return jax.shard_map(
        functools.partial(per_device, sizes),
        mesh=mesh,
        in_specs=(P("light", "depth", "tile"), P(), P(), P()),
        out_specs=(P(None, ("light", "depth"), "tile"), P(None, ("light", "depth"), "tile")),
        check_vma=False,
    )
```
